512 devices in a mesh: grp: 4 (over z_hi, core), blk: 32 (over x, z_lo), tp: 4 (over y).
Axes of the slice: x: 4, y: 4, z: 16 (z_hi: 2, z_lo: 8; z = z_hi * 8 + z_lo), core: 2. Of those that a mesh axis runs over, the one named last changes fastest.
Arguments:
- hidden_in: bfloat16 [16384, 4096], P(('grp', 'blk')), may hold values from -24 to 24
- value_weight: bfloat16 [4096, 512], P('blk', 'tp'), may hold values from -0.09375 to 0.09375
- queries: bfloat16 [16384, 4096], P(('grp', 'blk'), 'tp'), may hold values from -30 to 30
- key_vectors: bfloat16 [16384, 512], P(('grp', 'blk'), 'tp'), may hold values from -6 to 6
- cotangent: bfloat16 [16384, 4096], P(('grp', 'blk'), 'tp'), may hold values from -0.0625 to 0.0625
- doc_ids: int32 [16384], P(('grp', 'blk')), may hold values from 0 to 4095, as said below
- positions: int32 [16384], P(('grp', 'blk')), may hold values from 0 to 4095, as said below
Outputs:
- attended: bfloat16 [16384, 4096], P(('grp', 'blk'), 'tp')
- value_grad: float32 [4096, 512], P(('grp', 'blk'), 'tp')
The draws below stay inside these ranges and needn't reach their ends.
Inputs may be any that keep to these rules, and one draw needn't show every extreme that they name: `doc_ids`: the first group of 4096 tokens is one document; in every other group each document lies within the 128 tokens of one device, with ids unique within the group. Within a document positions count up from 0 in token order, except in the first group, where the devices' blocks of 128 positions follow an order given by a permutation of the devices.
All inputs are finite; a program needn't handle non-finite values.
Results may differ from the reference program's by a relative error of at most 0.017.
Values may be sent and summed in bfloat16 or wider, within the bound.
A program may use at most 64 MiB of HBM per device.

```python
import jax
import jax.numpy as jnp
from jax import lax

D = 4096
HQ = 32
KVH = 4
HD = 128
TOK_DEV = 128
TRACE = 4096
TOKENS = 16384


def shared_keys(key, spread, tie_factor):
    normal_part = jnp.clip(jax.random.normal(jax.random.fold_in(key, 101), (TOKENS, KVH * HD), jnp.float32), -6.0, 6.0)
    sample = normal_part
    row_scale = jnp.exp(spread * jax.random.uniform(jax.random.fold_in(key, 103), (TOKENS, 1), jnp.float32, -1.0, 1.0))
    in_block = (jnp.arange(TOKENS) % TOK_DEV)[:, None]
    row_scale = jnp.where(in_block < 2, 1.0, row_scale)
    sample = sample * row_scale
    blocked = sample.reshape(TOKENS // TOK_DEV, TOK_DEV, KVH * HD)
    leading = blocked[:, 0:1, :]
    slot = jnp.arange(TOK_DEV)[None, :, None]
    tied = jnp.where((slot == 1) & (tie_factor > 0.0), tie_factor * leading, blocked)
    return tied.reshape(TOKENS, KVH * HD)


def draw_key_vectors(key, part):
    sample = shared_keys(key, 0.0, 0.0)
    return sample.astype(jnp.bfloat16)


def draw_queries(key, part):
    key = jax.random.fold_in(key, 5)
    sample = jnp.clip(jax.random.normal(key, (TOKENS, HQ * HD), jnp.float32), -6.0, 6.0)
    return sample.astype(jnp.bfloat16)


def packing_layout(key):
    device_count = TOKENS // TOK_DEV
    cycle_length = TRACE // TOK_DEV
    block_order = jax.random.permutation(jax.random.fold_in(key, 201), cycle_length).astype(jnp.int32)
    marks = jax.random.randint(jax.random.fold_in(key, 202), (device_count, TOK_DEV), 0, 12)
    slot = jnp.arange(TOK_DEV, dtype=jnp.int32)[None, :]
    device = jnp.arange(device_count, dtype=jnp.int32)[:, None]
    fresh = (marks == 0) | (slot == 0) | (slot == TOK_DEV - 1)
    doc_start = lax.cummax(jnp.where(fresh, slot, 0), axis=1)
    cycle_index = device % cycle_length
    in_trace = device < cycle_length
    documents = jnp.where(in_trace, 0, cycle_index * TOK_DEV + doc_start)
    spots = jnp.where(in_trace, block_order[cycle_index] * TOK_DEV + slot, slot - doc_start)
    return (documents.reshape(TOKENS).astype(jnp.int32), spots.reshape(TOKENS).astype(jnp.int32))


def draw_doc_ids(key, part):
    documents, spots = packing_layout(key)
    return documents


def draw_positions(key, part):
    documents, spots = packing_layout(key)
    return spots


def with_spikes(drawn, key, source, target, shards_of, factor):
    def block_of(axis_at):
        return (jnp.arange(drawn.shape[axis_at]) // (drawn.shape[axis_at] // shards_of)).reshape((-1,) + (1,) * (drawn.ndim - 1 - axis_at))

    near = jax.random.permutation(key, shards_of)[block_of(target)]
    far = (block_of(target) + shards_of // 2) % shards_of
    return jnp.where((block_of(source) == near) | (block_of(source) == far), factor * drawn, drawn)


def steps_of(stream_key, dims, cuts, smallest, high):
    level = 1.0
    for axis_at, parts in cuts:
        draws = jax.random.uniform(jax.random.fold_in(jax.random.fold_in(stream_key, 6), axis_at), (parts,), jnp.float32, smallest / len(cuts), high / len(cuts))
        level = level * jnp.repeat(jnp.exp(draws), dims[axis_at] // parts).reshape((-1,) + (1,) * (len(dims) - 1 - axis_at))
    return level


def bell_draw(key, dims, scale, bound, split=(), kind=jnp.bfloat16):
    gain = steps_of(key, dims, split, -0.22, 0.18) if split else 1.0
    drawn = jax.random.normal(key, dims, jnp.float32) * scale * gain
    return jnp.minimum(jnp.maximum(drawn, -bound), bound).astype(kind)


def bell_draw_with(stream_key, extent, scale, reach, cuts, heavy, held_as=jnp.bfloat16):
    entries = scale * jax.random.normal(stream_key, extent, jnp.float32)
    if cuts:
        entries = entries * steps_of(stream_key, extent, cuts, -0.22, 0.18)
    return jnp.clip(with_spikes(entries, jax.random.fold_in(stream_key, 3), *heavy), -reach, reach).astype(held_as)


def setup_inputs(seed: int = 0) -> dict:
    arg_keys = jax.random.split(jax.random.key(seed), 8)
    return {
        "hidden_in": bell_draw_with(arg_keys[0], (TOKENS, D), 1.0, 24.0, ((0, 128),), (0, 1, 128, 5.5)),
        "value_weight": bell_draw(arg_keys[1], (D, KVH * HD), D ** -0.5, 0.09375, ((0, 32), (1, 4))),
        "queries": draw_queries(jax.random.fold_in(arg_keys[7], 71), 0),
        "key_vectors": draw_key_vectors(jax.random.fold_in(arg_keys[7], 71), 0),
        "cotangent": bell_draw(arg_keys[4], (TOKENS, HQ * HD), 0.01, 0.0625, ((0, 128), (1, 4))),
        "doc_ids": draw_doc_ids(jax.random.fold_in(arg_keys[7], 71), 0),
        "positions": draw_positions(jax.random.fold_in(arg_keys[7], 71), 0),
    }


def reference(hidden_in, value_weight, queries, key_vectors, cotangent, doc_ids, positions):
    group_size = HQ // KVH
    score_scale = HD ** -0.5
    num_groups = TOKENS // TRACE
    num_blocks = TRACE // TOK_DEV
    values = jnp.dot(hidden_in, value_weight, preferred_element_type=jnp.float32).astype(jnp.bfloat16)

    def per_head(q_head, k_head, v_head, c_head, g_docs, g_spots):
        q_blocks = q_head.reshape(num_blocks, TOK_DEV * group_size, HD)
        c_blocks = c_head.reshape(num_blocks, TOK_DEV * group_size, HD)
        d_blocks = jnp.repeat(g_docs, group_size).reshape(num_blocks, TOK_DEV * group_size)
        p_blocks = jnp.repeat(g_spots, group_size).reshape(num_blocks, TOK_DEV * group_size)

        def advance(grad_total, pieces):
            q_blk, c_blk, d_blk, p_blk = pieces
            scores = jnp.dot(q_blk, k_head.T, preferred_element_type=jnp.float32) * score_scale
            visible = (d_blk[:, None] == g_docs[None, :]) & (g_spots[None, :] <= p_blk[:, None])
            highest = jnp.max(jnp.where(visible, scores, -1e30), axis=1, keepdims=True)
            norm_sum = jnp.sum(jnp.where(visible, jnp.exp(scores - highest), 0.0), axis=1, keepdims=True)
            log_norm = highest + jnp.log(norm_sum)
            weights = jnp.where(visible, jnp.exp(scores - log_norm), 0.0).astype(jnp.bfloat16)
            out_blk = jnp.dot(weights, v_head, preferred_element_type=jnp.float32).astype(jnp.bfloat16)
            term = jnp.dot(weights.T, c_blk, preferred_element_type=jnp.float32).astype(jnp.bfloat16)
            term = lax.optimization_barrier(term)
            return grad_total + term.astype(jnp.float32), out_blk

        grad_total, outputs = lax.scan(advance, jnp.zeros((TRACE, HD), jnp.float32),
                                       (q_blocks, c_blocks, d_blocks, p_blocks))
        return outputs.reshape(TRACE, group_size * HD), grad_total

    def per_group(pieces):
        g_in, g_q, g_k, g_v, g_c, g_docs, g_spots = pieces
        q_heads = g_q.reshape(TRACE, KVH, group_size * HD).transpose(1, 0, 2)
        c_heads = g_c.reshape(TRACE, KVH, group_size * HD).transpose(1, 0, 2)
        k_heads = g_k.reshape(TRACE, KVH, HD).transpose(1, 0, 2)
        v_heads = g_v.reshape(TRACE, KVH, HD).transpose(1, 0, 2)

        def one_head(head_args):
            return per_head(head_args[0], head_args[1], head_args[2], head_args[3], g_docs, g_spots)

        outputs, grads = lax.map(one_head, (q_heads, k_heads, v_heads, c_heads))
        attended = outputs.transpose(1, 0, 2).reshape(TRACE, HQ * HD)
        value_grads = grads.transpose(1, 0, 2).reshape(TRACE, KVH * HD).astype(jnp.bfloat16)
        weight_grad = jnp.dot(g_in.T, value_grads, preferred_element_type=jnp.float32)
        return attended, weight_grad

    stacked = (hidden_in.reshape(num_groups, TRACE, D),
               queries.reshape(num_groups, TRACE, HQ * HD),
               key_vectors.reshape(num_groups, TRACE, KVH * HD),
               values.reshape(num_groups, TRACE, KVH * HD),
               cotangent.reshape(num_groups, TRACE, HQ * HD),
               doc_ids.reshape(num_groups, TRACE),
               positions.reshape(num_groups, TRACE))
    attended, weight_grads = lax.map(per_group, stacked)
    return attended.reshape(TOKENS, HQ * HD), jnp.sum(weight_grads, axis=0)
```

```python
import functools
import math

import jax
import jax.numpy as jnp
from jax import lax
from jax.experimental import pallas as pl
from jax.experimental.pallas import tpu as pltpu
from jax.sharding import PartitionSpec as P

HD = 128
NX = 4
NZ = 8
TOK = 128
SCALE = HD ** (-0.5) * math.log2(math.e)
HIDDEN = -1e30
MESH = pl.DeviceIdType.MESH
BF = jnp.bfloat16
F32 = jnp.float32
NT = (((1,), (1,)), ((), ()))


def wait_for(ref, sem):
    pltpu.make_async_copy(ref, ref, sem).wait()


def flip(row, rows):
    return jnp.transpose(jnp.broadcast_to(row, (rows, row.shape[1])))


def stack_pair(block):
    return jnp.concatenate([block[:, :HD], block[:, HD:]], axis=0)


def kernel(
    hid, wgt, qry, key, cot, doc, pos,
    att, grad,
    posb, Ws, Hs, HsT, Kb, Kpos, KposT, Qb, Qpos, Cb, Qf, Cf, Sb, Pm, ML, Wr, Cs,
    Vp, Vr, Vb, VT, Tsend, Tsib, Tz, Tr, Vg, Ost, Or, Gst, Gr,
    ssem, rsem, lsem,
):
    grp = lax.axis_index("grp")
    blk = lax.axis_index("blk")
    tp = lax.axis_index("tp")
    zh, c = grp // 2, grp % 2
    x, z = blk // NZ, blk % NZ
    me = x * 2 + c
    z16 = zh * NZ + z
    trace = zh == 0
    not_trace = zh != 0
    main = jnp.logical_and(trace, c == 0)
    side = jnp.logical_and(trace, c == 1)
    local = jnp.logical_not(main)
    owner = jnp.where(trace, z // 4 == c, c == 0)
    trace_owner = jnp.logical_and(trace, z // 4 == c)
    w_self = jnp.logical_and(jnp.logical_and(c == x % 2, z // 2 == x), z % 2 == c)

    def dev(x_, z_, zh_, c_):
        return (zh_ * 2 + c_, x_ * NZ + z_, tp)

    def put(src, dst, phase, to):
        pltpu.make_async_remote_copy(
            src_ref=src, dst_ref=dst, send_sem=ssem.at[phase], recv_sem=rsem.at[phase],
            device_id=to, device_id_type=MESH,
        ).start()

    near = []
    for k in (1, 2, 7, 6, 3, 5, 4):
        s = (me + k) % 8
        near.append((s // 2, s % 2))
    sib = dev(x, z, zh, 1 - c)
    line = [(z + k) % NZ for k in (4, 3, 5, 2, 6, 1, 7)]

    bar = pltpu.get_barrier_semaphore()

    def greet(to):
        pl.semaphore_signal(bar, inc=1, device_id=to, device_id_type=MESH)

    for xs, cs in near:
        greet(dev(xs, z, zh, cs))
    for k in range(1, 16):
        zz = (z16 + k) % 16
        greet(dev(x, zz % NZ, zz // NZ, c))
    for gi in range(2):
        for j in range(2):
            xw = c + 2 * gi
            zw = 2 * x + j
            same = jnp.logical_and(w_self, jnp.logical_and(xw == x, zw == z))

            @pl.when(jnp.logical_not(same))
            def _():
                greet(dev(xw, zw, zh, z % 2))

    HQD = 512
    pltpu.make_async_copy(
        hid.at[:, pl.ds(pl.multiple_of(c * 1024 + x * 256, 256), 256)],
        Hs.at[me, :, pl.ds(0, 256)], lsem.at[0]).start()
    pltpu.make_async_copy(
        hid.at[:, pl.ds(pl.multiple_of((c + 2) * 1024 + x * 256, 256), 256)],
        Hs.at[me, :, pl.ds(256, 256)], lsem.at[1]).start()

    @pl.when(main)
    def _():
        pltpu.make_async_copy(qry.at[:, pl.ds(0, HQD)], Qb.at[x], lsem.at[2]).start()
        pltpu.make_async_copy(cot.at[:, pl.ds(0, HQD)], Cb.at[x], lsem.at[3]).start()

    @pl.when(local)
    def _():
        pltpu.make_async_copy(qry, Qf, lsem.at[4]).start()
        pltpu.make_async_copy(cot, Cf, lsem.at[5]).start()

    posb[...] = jnp.broadcast_to(pos[...], (8, TOK))

    @pl.when(main)
    def _():
        Kb[pl.ds(pl.multiple_of(z * TOK, TOK), TOK), :] = key[...]
        Kpos[z] = posb[...]
        Qpos[x] = posb[...]

    pl.semaphore_wait(bar, 22 + 4 - w_self.astype(jnp.int32))

    @pl.when(main)
    def _():
        for zz in line:
            put(key, Kb.at[pl.ds(pl.multiple_of(z * TOK, TOK), TOK), :], 0, dev(x, zz, zh, 0))
        for zz in line:
            put(posb, Kpos.at[z], 1, dev(x, zz, zh, 0))
        for xs, cs in near:
            to = dev(xs, z, zh, cs)
            put(qry.at[:, pl.ds(pl.multiple_of(cs * HQD, HQD), HQD)], Qb.at[x], 2, to)
            put(posb, Qpos.at[x], 3, to)

    slot = (x // 2) * 2 + z % 2
    for i in range(4):
        zt = 2 * i + c
        same = jnp.logical_and(w_self, zt == z)

        @pl.when(jnp.logical_not(same))
        def _():
            put(wgt, Ws.at[pl.ds(pl.multiple_of(slot * TOK, TOK), TOK), :], 4,
                dev(z // 2, zt, zh, x % 2))

    @pl.when(w_self)
    def _():
        pltpu.make_async_copy(
            wgt, Ws.at[pl.ds(pl.multiple_of(slot * TOK, TOK), TOK), :], rsem.at[4]).start()

    for xs, cs in near:
        to = dev(xs, z, zh, cs)
        for gi in range(2):
            col = pl.multiple_of((cs + 2 * gi) * 1024 + xs * 256, 256)
            put(hid.at[:, pl.ds(col, 256)], Hs.at[me, :, pl.ds(gi * 256, 256)], 5, to)

    @pl.when(main)
    def _():
        for xs, cs in near:
            put(cot.at[:, pl.ds(pl.multiple_of(cs * HQD, HQD), HQD)], Cb.at[x], 6,
                dev(xs, z, zh, cs))

    @pl.when(trace)
    def _():
        @pl.when(c == 0)
        def _():
            wait_for(Kb.at[pl.ds(0, 7 * TOK), :], rsem.at[0])
            put(Kb, Kb, 16, sib)
            wait_for(Kpos.at[pl.ds(0, 7)], rsem.at[1])
            put(Kpos, Kpos, 17, sib)
            wait_for(Qb.at[pl.ds(0, 3)], rsem.at[2])
            wait_for(Qpos.at[pl.ds(0, 3)], rsem.at[3])
            wait_for(Qb.at[0], lsem.at[2])

        @pl.when(c == 1)
        def _():
            wait_for(Kb, rsem.at[16])
            wait_for(Kpos, rsem.at[17])
            wait_for(Qb, rsem.at[2])
            wait_for(Qpos, rsem.at[3])

        for t in range(NZ):
            KposT[pl.ds(t * TOK, TOK), :] = flip(Kpos[t, 0:1, :].astype(F32), TOK)

        def score_block(xq, carry):
            q_at = Qpos[xq][0:1, :].astype(F32)
            tops, sums = [], []
            for pair in range(2):
                qp = stack_pair(Qb[xq, :, pl.ds(pair * 256, 256)])
                top = jnp.full((8, 256), HIDDEN, F32)
                for t in range(4):
                    rows = pl.ds(t * 256, 256)
                    s = lax.dot_general(Kb[rows, :], qp, NT, preferred_element_type=F32)
                    seen = KposT[rows, :] <= q_at
                    s = jnp.concatenate(
                        [jnp.where(seen, s[:, :HD], HIDDEN), jnp.where(seen, s[:, HD:], HIDDEN)],
                        axis=1)
                    Sb[rows, :] = s
                    top = jnp.maximum(top, jnp.max(s.reshape(32, 8, 256), axis=0))
                m = jnp.max(top, axis=0, keepdims=True) * SCALE
                total = jnp.zeros((8, 256), F32)
                at = pl.ds(pl.multiple_of(xq * 512 + pair * 256, 256), 256)
                for t in range(8):
                    rows = pl.ds(t * TOK, TOK)
                    p = jnp.exp2(Sb[rows, :] * SCALE - m)
                    total = total + jnp.sum(p.reshape(16, 8, 256), axis=0)
                    Pm[rows, at] = p.astype(BF)
                tops.append(m)
                sums.append(jnp.sum(total, axis=0, keepdims=True))
            ML[x, xq] = jnp.concatenate(
                tops + sums + [jnp.zeros((4, 256), F32)], axis=0)
            return carry

        lax.fori_loop(0, NX, score_block, 0)
        for k in (1, 3, 2):
            put(ML.at[x], ML.at[x], 7, dev((x + k) % NX, z, zh, c))

    wait_for(Ws, rsem.at[4])
    wait_for(Hs.at[pl.ds(0, 7)], rsem.at[5])
    wait_for(Hs.at[0, :, pl.ds(0, 256)], lsem.at[0])
    wait_for(Hs.at[0, :, pl.ds(0, 256)], lsem.at[1])

    def value_part(s, carry):
        Vp[s] = jnp.dot(Hs[s], Ws[...], preferred_element_type=F32).astype(BF)
        return carry

    lax.fori_loop(0, 8, value_part, 0)
    for xs, cs in near:
        put(Vp.at[xs * 2 + cs], Vr.at[me], 8, dev(xs, z, zh, cs))
    Vr[me] = Vp[me]
    for s in range(8):
        HsT[:, pl.ds(s * TOK, TOK)] = jnp.transpose(Hs[s])

    @pl.when(trace)
    def _():
        wait_for(ML.at[pl.ds(0, 3)], rsem.at[7])

        @pl.when(c == 0)
        def _():
            wait_for(Cb.at[pl.ds(0, 3)], rsem.at[6])
            wait_for(Cb.at[0], lsem.at[3])

        @pl.when(c == 1)
        def _():
            wait_for(Cb, rsem.at[6])

        def scale_block(xq, carry):
            parts = [ML[s, xq] for s in range(NX)]
            high = functools.reduce(jnp.maximum, [p[0:2] for p in parts])
            total = functools.reduce(
                jnp.add, [p[2:4] * jnp.exp2(p[0:2] - high) for p in parts])
            w = jnp.exp2(ML[x, xq][0:2] - high) / total
            Wr[xq] = jnp.concatenate([w, jnp.zeros((6, 256), F32)], axis=0)
            for pair in range(2):
                cp = stack_pair(Cb[xq, :, pl.ds(pair * 256, 256)]).astype(F32)
                rows = pl.ds(pl.multiple_of(xq * 512 + pair * 256, 256), 256)
                Cs[rows, :] = (cp * flip(w[pair:pair + 1], TOK)).astype(BF)
            return carry

        lax.fori_loop(0, NX, scale_block, 0)
        theirs = pl.ds(pl.multiple_of((1 - c) * 512, 512), 512)
        ours = pl.ds(pl.multiple_of(c * 512, 512), 512)
        Tsend[...] = jnp.dot(Pm[theirs, :], Cs[...], preferred_element_type=F32).astype(BF)
        put(Tsend, Tsib, 9, sib)
        mine = jnp.dot(Pm[ours, :], Cs[...], preferred_element_type=F32)
        wait_for(Tsib, rsem.at[9])
        Tz[...] = (mine + Tsib[...].astype(F32)).astype(BF).reshape(4, TOK, HD)
        for k in range(4):
            zt = 4 * c + k

            @pl.when(zt != z)
            def _():
                put(Tz.at[k], Tr.at[z], 10, dev(x, zt, zh, c))

            @pl.when(zt == z)
            def _():
                Tr[z] = Tz[k]

    wait_for(Vr.at[pl.ds(0, 7)], rsem.at[8])
    val = functools.reduce(jnp.add, [Vr[s].astype(F32) for s in range(8)]).astype(BF)

    @pl.when(main)
    def _():
        rows = pl.ds(pl.multiple_of(z * TOK, TOK), TOK)
        Vb[rows, :] = val
        for zz in line:
            put(Vb.at[rows, :], Vb.at[rows, :], 11, dev(x, zz, zh, 0))

    @pl.when(local)
    def _():
        wait_for(Qf, lsem.at[4])
        wait_for(Cf, lsem.at[5])
        val_t = jnp.transpose(val)
        p_row = pos[...].astype(F32)
        d_row = doc[...].astype(F32)
        seen = jnp.logical_and(flip(p_row, TOK) <= p_row, flip(d_row, TOK) == d_row)
        terms = jnp.zeros((TOK, HD), F32)
        for pair in range(4):
            qp = stack_pair(Qf[:, pl.ds(pair * 256, 256)])
            s = lax.dot_general(key[...], qp, NT, preferred_element_type=F32)
            s = jnp.concatenate(
                [jnp.where(seen, s[:, :HD], HIDDEN), jnp.where(seen, s[:, HD:], HIDDEN)], axis=1)
            s = s * SCALE
            p = jnp.exp2(s - jnp.max(s, axis=0, keepdims=True))
            w = 1.0 / jnp.sum(p, axis=0, keepdims=True)
            pb = (p * w).astype(BF)
            o = jnp.dot(val_t, pb, preferred_element_type=F32)
            att[:, pl.ds(pair * 256, HD)] = jnp.transpose(o[:, :HD]).astype(BF)
            att[:, pl.ds(pair * 256 + HD, HD)] = jnp.transpose(o[:, HD:]).astype(BF)
            cp = stack_pair(Cf[:, pl.ds(pair * 256, 256)])
            terms = terms + jnp.dot(pb, cp, preferred_element_type=F32)
        Vg[me] = terms.astype(BF)
        for phase, core in ((12, 0), (13, 1)):
            @pl.when(c == core)
            def _():
                for xs, cs in near:
                    put(Vg.at[me], Vg.at[me], phase, dev(xs, z, zh, cs))

    @pl.when(trace_owner)
    def _():
        wait_for(Tr.at[pl.ds(0, 7)], rsem.at[10])
        Vg[2 * x] = functools.reduce(
            jnp.add, [Tr[s].astype(F32) for s in range(NZ)]).astype(BF)
        for xs, cs in near:
            put(Vg.at[2 * x], Vg.at[2 * x], 12, dev(xs, z, zh, cs))

    for phase, sender in ((12, owner), (13, c == 1)):
        @pl.when(sender)
        def _():
            wait_for(Vg.at[pl.ds(0, 3)], rsem.at[phase])

        @pl.when(jnp.logical_not(sender))
        def _():
            wait_for(Vg.at[pl.ds(0, 4)], rsem.at[phase])

    vg_all = Vg[...].reshape(8 * TOK, HD)
    Gst[...] = jnp.dot(HsT[...], vg_all, preferred_element_type=F32).astype(BF).reshape(16, 32, HD)
    for k in (8, 7, 9, 6, 10, 5, 11, 4, 12, 3, 13, 2, 14, 1, 15):
        zz = (z16 + k) % 16
        put(Gst.at[zz], Gr.at[z16], 14, dev(x, zz % NZ, zz // NZ, c))
    Gr[z16] = Gst[z16]

    @pl.when(trace)
    def _():
        @pl.when(c == 0)
        def _():
            wait_for(Vb.at[pl.ds(0, 7 * TOK), :], rsem.at[11])
            put(Vb, Vb, 18, sib)

        @pl.when(c == 1)
        def _():
            wait_for(Vb, rsem.at[18])

        VT[...] = jnp.transpose(Vb[...])

        def out_block(xq, carry):
            w = Wr[xq]
            for pair in range(2):
                at = pl.ds(pl.multiple_of(xq * 512 + pair * 256, 256), 256)
                o = jnp.dot(VT[...], Pm[:, at], preferred_element_type=F32) * w[pair:pair + 1]
                Ost[xq, pl.ds(pair * 256, 256), :] = jnp.transpose(o).astype(BF)
            return carry

        lax.fori_loop(0, NX, out_block, 0)
        for k in range(NX):
            xt = (x + k) % NX
            if k == 0:
                @pl.when(c == 1)
                def _():
                    put(Ost.at[x], Or.at[me], 15, sib)

                @pl.when(c == 0)
                def _():
                    Or[me] = Ost[x]
            else:
                put(Ost.at[xt], Or.at[me], 15, dev(xt, z, zh, 0))

    @pl.when(main)
    def _():
        wait_for(Or.at[pl.ds(0, 7)], rsem.at[15])
        for half in range(2):
            for h in range(4):
                o = functools.reduce(
                    jnp.add, [Or[2 * s + half, pl.ds(h * TOK, TOK), :].astype(F32) for s in range(NX)])
                att[:, pl.ds((half * 4 + h) * HD, HD)] = o.astype(BF)

    wait_for(Gr.at[pl.ds(0, 15)], rsem.at[14])
    grad[...] = functools.reduce(jnp.add, [Gr[s].astype(F32) for s in range(16)])

    @pl.when(main)
    def _():
        wait_for(Kb.at[pl.ds(0, 7 * TOK), :], ssem.at[0])
        wait_for(Kb, ssem.at[16])
        wait_for(Kpos.at[pl.ds(0, 7)], ssem.at[1])
        wait_for(Kpos, ssem.at[17])
        wait_for(Or.at[pl.ds(0, 7)], ssem.at[2])
        wait_for(Kpos.at[pl.ds(0, 7)], ssem.at[3])
        wait_for(Or.at[pl.ds(0, 7)], ssem.at[6])
        wait_for(Vb.at[pl.ds(0, 7 * TOK), :], ssem.at[11])
        wait_for(Vb, ssem.at[18])
        wait_for(Ost.at[pl.ds(0, 3)], ssem.at[15])

    @pl.when(side)
    def _():
        wait_for(Ost, ssem.at[15])

    @pl.when(w_self)
    def _():
        wait_for(Ws.at[pl.ds(0, 3 * TOK), :], ssem.at[4])

    @pl.when(jnp.logical_not(w_self))
    def _():
        wait_for(Ws, ssem.at[4])

    wait_for(Hs.at[pl.ds(0, 7)], ssem.at[5])

    @pl.when(trace)
    def _():
        wait_for(ML.at[pl.ds(0, 3)], ssem.at[7])
        wait_for(Tsend, ssem.at[9])

    @pl.when(trace_owner)
    def _():
        wait_for(Tz.at[pl.ds(0, 3)], ssem.at[10])

    @pl.when(jnp.logical_and(trace, jnp.logical_not(trace_owner)))
    def _():
        wait_for(Tz, ssem.at[10])

    wait_for(Vr.at[pl.ds(0, 7)], ssem.at[8])

    @pl.when(owner)
    def _():
        wait_for(Vg.at[pl.ds(0, 7)], ssem.at[12])

    @pl.when(c == 1)
    def _():
        wait_for(Vg.at[pl.ds(0, 7)], ssem.at[13])

    wait_for(Gr.at[pl.ds(0, 15)], ssem.at[14])


def per_device(hidden_in, value_weight, queries, key_vectors, cotangent, doc_ids, positions):
    vmem = pl.BlockSpec(memory_space=pltpu.VMEM)
    anywhere = pl.BlockSpec(memory_space=pl.ANY)
    scratch = [
        pltpu.VMEM((8, TOK), jnp.int32),
        pltpu.VMEM((512, HD), BF),
        pltpu.VMEM((8, TOK, 512), BF),
        pltpu.VMEM((512, 1024), BF),
        pltpu.VMEM((1024, HD), BF),
        pltpu.VMEM((8, 8, TOK), jnp.int32),
        pltpu.VMEM((1024, TOK), F32),
        pltpu.VMEM((NX, TOK, 512), BF),
        pltpu.VMEM((NX, 8, TOK), jnp.int32),
        pltpu.VMEM((NX, TOK, 512), BF),
        pltpu.VMEM((TOK, 1024), BF),
        pltpu.VMEM((TOK, 1024), BF),
        pltpu.VMEM((1024, 256), F32),
        pltpu.VMEM((1024, 2048), BF),
        pltpu.VMEM((NX, NX, 8, 256), F32),
        pltpu.VMEM((NX, 8, 256), F32),
        pltpu.VMEM((2048, HD), BF),
        pltpu.VMEM((8, TOK, HD), BF),
        pltpu.VMEM((8, TOK, HD), BF),
        pltpu.VMEM((1024, HD), BF),
        pltpu.VMEM((HD, 1024), BF),
        pltpu.VMEM((512, HD), BF),
        pltpu.VMEM((512, HD), BF),
        pltpu.VMEM((4, TOK, HD), BF),
        pltpu.VMEM((8, TOK, HD), BF),
        pltpu.VMEM((8, TOK, HD), BF),
        pltpu.VMEM((NX, 512, HD), BF),
        pltpu.VMEM((2 * NX, 512, HD), BF),
        pltpu.VMEM((16, 32, HD), BF),
        pltpu.VMEM((16, 32, HD), BF),
        pltpu.SemaphoreType.DMA((19,)),
        pltpu.SemaphoreType.DMA((19,)),
        pltpu.SemaphoreType.DMA((6,)),
    ]
    return pl.pallas_call(
        kernel,
        name="trace_attention",
        out_shape=(
            jax.ShapeDtypeStruct((TOK, 1024), BF),
            jax.ShapeDtypeStruct((32, HD), F32),
        ),
        in_specs=[anywhere, vmem, anywhere, vmem, anywhere, vmem, vmem],
        out_specs=(vmem, vmem),
        scratch_shapes=scratch,
        compiler_params=pltpu.CompilerParams(
            collective_id=0, has_side_effects=True, vmem_limit_bytes=40 << 20
        ),
    )(
        hidden_in, value_weight, queries, key_vectors, cotangent,
        doc_ids.reshape(1, TOK), positions.reshape(1, TOK),
    )


def solution(mesh):
    in_specs = (
        P(("grp", "blk"), None),
        P("blk", "tp"),
        P(("grp", "blk"), "tp"),
        P(("grp", "blk"), "tp"),
        P(("grp", "blk"), "tp"),
        P(("grp", "blk")),
        P(("grp", "blk")),
    )
    out_specs = (P(("grp", "blk"), "tp"), P(("grp", "blk"), "tp"))
    return jax.shard_map(
        per_device, mesh=mesh, in_specs=in_specs, out_specs=out_specs, check_vma=False
    )
```

```python
import functools
import math

import jax
import jax.numpy as jnp
from jax import lax
from jax.experimental import pallas as pl
from jax.experimental.pallas import tpu as pltpu
from jax.sharding import PartitionSpec as P

HD = 128
NX = 4
NZ = 8
TOK = 128
SCALE = HD ** (-0.5) * math.log2(math.e)
HIDDEN = -1e30
MESH = pl.DeviceIdType.MESH
BF = jnp.bfloat16
F32 = jnp.float32
NT = (((1,), (1,)), ((), ()))


def wait_for(ref, sem):
    pltpu.make_async_copy(ref, ref, sem).wait()


def flip(row, rows):
    return jnp.transpose(jnp.broadcast_to(row, (rows, row.shape[1])))


def stack_pair(block):
    return jnp.concatenate([block[:, :HD], block[:, HD:]], axis=0)


def kernel(
    hid, wgt, qry, key, cot, doc, pos,
    att, grad,
    posv, docv, posb, Kv, Wg, Hf, Hs, HsT, Kx, KposT, Qb, Qpos, Cb, Qf, Cf, Sb, Pm, ML, Wr, Cs,
    Vp, Vs, Vb, VT, Tsend, Tsib, Tz, Tr, Vg, Ost, Or, Ah, Gst, Gr,
    ssem, rsem, lsem, far_in,
):
    grp = lax.axis_index("grp")
    blk = lax.axis_index("blk")
    tp = lax.axis_index("tp")
    zh, c = grp // 2, grp % 2
    x, z = blk // NZ, blk % NZ
    me = x * 2 + c
    z16 = zh * NZ + z
    trace = zh == 0
    main = jnp.logical_and(trace, c == 0)
    side = jnp.logical_and(trace, c == 1)
    local = jnp.logical_not(main)
    half_owner = z // 4 == c
    owner = jnp.where(trace, half_owner, c == 0)
    trace_owner = jnp.logical_and(trace, half_owner)

    def dev(x_, z_, zh_, c_):
        return (zh_ * 2 + c_, x_ * NZ + z_, tp)

    def put(src, dst, phase, to):
        pltpu.make_async_remote_copy(
            src_ref=src, dst_ref=dst, send_sem=ssem.at[phase], recv_sem=rsem.at[phase],
            device_id=to, device_id_type=MESH,
        ).start()

    near = []
    for k in (1, 2, 7, 6, 3, 5, 4):
        s = (me + k) % 8
        near.append((s // 2, s % 2))
    sib = dev(x, z, zh, 1 - c)
    line = [(z + k) % NZ for k in (4, 3, 5, 2, 6, 1, 7)]
    ring = [(x + k) % NX for k in (2, 1, 3)]
    half = pl.multiple_of(c * 512, 512)

    bar = pltpu.get_barrier_semaphore()

    def greet(to):
        pl.semaphore_signal(bar, inc=1, device_id=to, device_id_type=MESH)

    for xs, cs in near:
        greet(dev(xs, z, zh, cs))
    for zz in line:
        greet(dev(x, zz, zh, c))

    @pl.when(trace)
    def _():
        for zz in range(NZ):
            greet(dev(x, zz, 1, c))

    pltpu.make_async_copy(key, Kv.at[pl.ds(0, TOK), :], lsem.at[6]).start()
    pltpu.make_async_copy(pos, posv, lsem.at[7]).start()
    pltpu.make_async_copy(doc, docv, lsem.at[8]).start()
    for k in range(NX):
        pltpu.make_async_copy(
            hid.at[:, pl.ds(pl.multiple_of(k * 1024 + half, 512), 512)],
            Hf.at[c, :, pl.ds(k * 512, 512)], lsem.at[0]).start()
    for gi in range(2):
        pltpu.make_async_copy(
            hid.at[:, pl.ds(pl.multiple_of((c + 2 * gi) * 1024 + x * 256, 256), 256)],
            Hs.at[me, :, pl.ds(gi * 256, 256)], lsem.at[1]).start()

    @pl.when(main)
    def _():
        pltpu.make_async_copy(qry.at[:, pl.ds(0, 512)], Qb.at[x], lsem.at[2]).start()
        pltpu.make_async_copy(cot.at[:, pl.ds(0, 512)], Cb.at[x], lsem.at[3]).start()

    @pl.when(local)
    def _():
        pltpu.make_async_copy(qry, Qf, lsem.at[4]).start()
        pltpu.make_async_copy(cot, Cf, lsem.at[5]).start()

    wait_for(Kv.at[pl.ds(0, TOK), :], lsem.at[6])
    wait_for(posv, lsem.at[7])
    wait_for(docv, lsem.at[8])
    posb[...] = jnp.broadcast_to(posv[...], (8, TOK))
    p_row = posv[...].astype(F32)
    p_high = jnp.floor(p_row * (1.0 / 64.0))
    Kv[pl.ds(TOK, 16), :] = jnp.concatenate(
        [jnp.broadcast_to(p_high, (8, TOK)), jnp.broadcast_to(p_row - 64.0 * p_high, (8, TOK))],
        axis=0).astype(BF)

    @pl.when(main)
    def _():
        Kx[z] = Kv[...]
        Qpos[x] = posb[...]

    pl.semaphore_wait(bar, jnp.where(trace, 14, 22))

    @pl.when(main)
    def _():
        put(qry.at[:, pl.ds(512, 512)], Qb.at[x], 19, sib)
        for zz in line:
            put(Kv, Kx.at[z], 0, dev(x, zz, zh, 0))
        for xt in ring:
            put(qry.at[:, pl.ds(0, 512)], Qb.at[x], 2, dev(xt, z, zh, 0))
        for xs, cs in near:
            put(posb, Qpos.at[x], 3, dev(xs, z, zh, cs))
        put(cot.at[:, pl.ds(512, 512)], Cb.at[x], 20, sib)

    slot = pl.ds(pl.multiple_of((z % 4) * TOK, TOK), TOK)

    @pl.when(half_owner)
    def _():
        pltpu.make_async_copy(wgt, Wg.at[x, slot, :], rsem.at[4]).start()
        for zz in line:
            put(wgt, Wg.at[x, slot, :], 4, dev(x, zz, zh, c))

    @pl.when(main)
    def _():
        for xt in ring:
            put(cot.at[:, pl.ds(0, 512)], Cb.at[x], 6, dev(xt, z, zh, 0))

    for k in range(NX):
        put(hid.at[:, pl.ds(pl.multiple_of(k * 1024 + (1 - c) * 512, 512), 512)],
            Hf.at[c, :, pl.ds(k * 512, 512)], 21, sib)

    @pl.when(zh != 0)
    def _():
        for zz in range(NZ):
            pl.semaphore_signal(
                far_in, inc=1, device_id=dev(x, zz, 0, c), device_id_type=MESH)

    @pl.when(side)
    def _():
        wait_for(Qb.at[0], rsem.at[19])
        for xt in ring:
            put(Qb.at[x], Qb.at[x], 2, dev(xt, z, zh, 1))
        wait_for(Cb.at[0], rsem.at[20])
        for xt in ring:
            put(Cb.at[x], Cb.at[x], 6, dev(xt, z, zh, 1))

    @pl.when(main)
    def _():
        wait_for(Kx.at[pl.ds(0, 7)], rsem.at[0])
        put(Kx, Kx, 16, sib)

    wait_for(Wg.at[0], rsem.at[4])
    for xt in ring:
        put(Wg.at[x], Wg.at[x], 17, dev(xt, z, zh, c))

    @pl.when(trace)
    def _():
        @pl.when(c == 0)
        def _():
            wait_for(Qpos.at[pl.ds(0, 3)], rsem.at[3])
            wait_for(Qb.at[0], lsem.at[2])

        @pl.when(c == 1)
        def _():
            wait_for(Kx, rsem.at[16])
            wait_for(Qpos.at[pl.ds(0, 4)], rsem.at[3])

        wait_for(Qb.at[pl.ds(0, 3)], rsem.at[2])

        for t in range(NZ):
            digits = Kx[t, pl.ds(TOK, 16), :].astype(F32)
            KposT[pl.ds(t * TOK, TOK), :] = flip(digits[0:1] * 64.0 + digits[8:9], TOK)

        def score_block(xq, carry):
            q_at = Qpos[xq][0:1, :].astype(F32)
            tops, sums = [], []
            for pair in range(2):
                qp = stack_pair(Qb[xq, :, pl.ds(pair * 256, 256)])
                top = jnp.full((8, 256), HIDDEN, F32)
                for t in range(4):
                    rows = pl.ds(t * 256, 256)
                    kk = jnp.concatenate(
                        [Kx[2 * t, pl.ds(0, TOK), :], Kx[2 * t + 1, pl.ds(0, TOK), :]], axis=0)
                    s = lax.dot_general(kk, qp, NT, preferred_element_type=F32)
                    seen = KposT[rows, :] <= q_at
                    s = jnp.concatenate(
                        [jnp.where(seen, s[:, :HD], HIDDEN), jnp.where(seen, s[:, HD:], HIDDEN)],
                        axis=1)
                    Sb[rows, :] = s
                    top = jnp.maximum(top, jnp.max(s.reshape(32, 8, 256), axis=0))
                m = jnp.max(top, axis=0, keepdims=True) * SCALE
                total = jnp.zeros((8, 256), F32)
                at = pl.ds(pl.multiple_of(xq * 512 + pair * 256, 256), 256)
                for t in range(8):
                    rows = pl.ds(t * TOK, TOK)
                    p = jnp.exp2(Sb[rows, :] * SCALE - m)
                    total = total + jnp.sum(p.reshape(16, 8, 256), axis=0)
                    Pm[rows, at] = p.astype(BF)
                tops.append(m)
                sums.append(jnp.sum(total, axis=0, keepdims=True))
            ML[x, xq] = jnp.concatenate(
                tops + sums + [jnp.zeros((4, 256), F32)], axis=0)
            return carry

        lax.fori_loop(0, NX, score_block, 0)
        for xt in ring:
            put(ML.at[x], ML.at[x], 7, dev(xt, z, zh, c))

    for xs, cs in near:
        for gi in range(2):
            col = pl.multiple_of((cs + 2 * gi) * 1024 + xs * 256, 256)
            put(hid.at[:, pl.ds(col, 256)], Hs.at[me, :, pl.ds(gi * 256, 256)], 5,
                dev(xs, z, zh, cs))

    wait_for(Wg.at[pl.ds(0, 3)], rsem.at[17])
    wait_for(Hf.at[0], lsem.at[0])
    wait_for(Hf.at[0], rsem.at[21])
    w_all = Wg[...].reshape(2048, HD)
    Vp[...] = jnp.dot(Hf[1 - c], w_all, preferred_element_type=F32)
    put(Vp, Vs, 8, sib)
    own_part = jnp.dot(Hf[c], w_all, preferred_element_type=F32)
    wait_for(Vs, rsem.at[8])
    val = (own_part + Vs[...]).astype(BF)

    @pl.when(main)
    def _():
        rows = pl.ds(pl.multiple_of(z * TOK, TOK), TOK)
        Vb[rows, :] = val
        for zz in line:
            put(Vb.at[rows, :], Vb.at[rows, :], 11, dev(x, zz, zh, 0))

    @pl.when(trace)
    def _():
        @pl.when(c == 0)
        def _():
            wait_for(Cb.at[0], lsem.at[3])

        wait_for(Cb.at[pl.ds(0, 3)], rsem.at[6])
        wait_for(ML.at[pl.ds(0, 3)], rsem.at[7])

        def scale_block(xq, carry):
            parts = [ML[s, xq] for s in range(NX)]
            high = functools.reduce(jnp.maximum, [p[0:2] for p in parts])
            total = functools.reduce(
                jnp.add, [p[2:4] * jnp.exp2(p[0:2] - high) for p in parts])
            w = jnp.exp2(ML[x, xq][0:2] - high) / total
            Wr[xq] = jnp.concatenate([w, jnp.zeros((6, 256), F32)], axis=0)
            for pair in range(2):
                cp = stack_pair(Cb[xq, :, pl.ds(pair * 256, 256)]).astype(F32)
                rows = pl.ds(pl.multiple_of(xq * 512 + pair * 256, 256), 256)
                Cs[rows, :] = (cp * flip(w[pair:pair + 1], TOK)).astype(BF)
            return carry

        lax.fori_loop(0, NX, scale_block, 0)
        theirs = pl.ds(pl.multiple_of((1 - c) * 512, 512), 512)
        ours = pl.ds(half, 512)
        Tsend[...] = jnp.dot(Pm[theirs, :], Cs[...], preferred_element_type=F32).astype(BF)
        put(Tsend, Tsib, 9, sib)
        mine = jnp.dot(Pm[ours, :], Cs[...], preferred_element_type=F32)
        wait_for(Tsib, rsem.at[9])
        Tz[...] = (mine + Tsib[...].astype(F32)).astype(BF).reshape(4, TOK, HD)
        for k in range(4):
            zt = 4 * c + k

            @pl.when(zt != z)
            def _():
                put(Tz.at[k], Tr.at[z], 10, dev(x, zt, zh, c))

            @pl.when(zt == z)
            def _():
                Tr[z] = Tz[k]

    @pl.when(local)
    def _():
        wait_for(Qf, lsem.at[4])
        wait_for(Cf, lsem.at[5])
        val_t = jnp.transpose(val)
        d_row = docv[...].astype(F32)
        seen = jnp.logical_and(flip(p_row, TOK) <= p_row, flip(d_row, TOK) == d_row)
        terms = jnp.zeros((TOK, HD), F32)
        for pair in range(4):
            qp = stack_pair(Qf[:, pl.ds(pair * 256, 256)])
            s = lax.dot_general(Kv[pl.ds(0, TOK), :], qp, NT, preferred_element_type=F32)
            s = jnp.concatenate(
                [jnp.where(seen, s[:, :HD], HIDDEN), jnp.where(seen, s[:, HD:], HIDDEN)], axis=1)
            s = s * SCALE
            p = jnp.exp2(s - jnp.max(s, axis=0, keepdims=True))
            w = 1.0 / jnp.sum(p, axis=0, keepdims=True)
            pb = (p * w).astype(BF)
            o = jnp.dot(val_t, pb, preferred_element_type=F32)
            att[:, pl.ds(pair * 256, HD)] = jnp.transpose(o[:, :HD]).astype(BF)
            att[:, pl.ds(pair * 256 + HD, HD)] = jnp.transpose(o[:, HD:]).astype(BF)
            cp = stack_pair(Cf[:, pl.ds(pair * 256, 256)])
            terms = terms + jnp.dot(pb, cp, preferred_element_type=F32)
        Vg[me] = terms.astype(BF)
        for phase, core in ((12, 0), (13, 1)):
            @pl.when(c == core)
            def _():
                for xs, cs in near:
                    put(Vg.at[me], Vg.at[me], phase, dev(xs, z, zh, cs))

    wait_for(Hs.at[pl.ds(0, 7)], rsem.at[5])
    wait_for(Hs.at[0], lsem.at[1])
    for s in range(8):
        HsT[:, pl.ds(s * TOK, TOK)] = jnp.transpose(Hs[s])

    @pl.when(main)
    def _():
        wait_for(Vb.at[pl.ds(0, 7 * TOK), :], rsem.at[11])
        put(Vb, Vb, 18, sib)

    @pl.when(trace_owner)
    def _():
        wait_for(Tr.at[pl.ds(0, 7)], rsem.at[10])
        Vg[2 * x] = functools.reduce(
            jnp.add, [Tr[s].astype(F32) for s in range(NZ)]).astype(BF)
        for xs, cs in near:
            put(Vg.at[2 * x], Vg.at[2 * x], 12, dev(xs, z, zh, cs))

    @pl.when(trace)
    def _():
        @pl.when(c == 1)
        def _():
            wait_for(Vb, rsem.at[18])

        VT[...] = jnp.transpose(Vb[...])

        def out_block(xq, carry):
            w = Wr[xq]
            for pair in range(2):
                at = pl.ds(pl.multiple_of(xq * 512 + pair * 256, 256), 256)
                o = jnp.dot(VT[...], Pm[:, at], preferred_element_type=F32) * w[pair:pair + 1]
                Ost[xq, pl.ds(pair * 256, 256), :] = jnp.transpose(o).astype(BF)
            return carry

        lax.fori_loop(0, NX, out_block, 0)
        for xt in ring:
            put(Ost.at[xt], Or.at[x], 15, dev(xt, z, zh, c))
        Or[x] = Ost[x]

    for phase, sender in ((12, owner), (13, c == 1)):
        @pl.when(sender)
        def _():
            wait_for(Vg.at[pl.ds(0, 3)], rsem.at[phase])

        @pl.when(jnp.logical_not(sender))
        def _():
            wait_for(Vg.at[pl.ds(0, 4)], rsem.at[phase])

    vg_all = Vg[...].reshape(8 * TOK, HD)
    Gst[...] = jnp.dot(HsT[...], vg_all, preferred_element_type=F32).astype(BF).reshape(16, 32, HD)

    @pl.when(trace)
    def _():
        pl.semaphore_wait(far_in, NZ)

    for k in (8, 7, 9, 6, 10, 5, 11, 4, 12, 3, 13, 2, 14, 1, 15):
        zz = (z16 + k) % 16
        put(Gst.at[zz], Gr.at[z16], 14, dev(x, zz % NZ, zz // NZ, c))
    Gr[z16] = Gst[z16]

    @pl.when(trace)
    def _():
        wait_for(Or.at[pl.ds(0, 3)], rsem.at[15])
        for h in range(4):
            o = functools.reduce(
                jnp.add, [Or[s, pl.ds(h * TOK, TOK), :].astype(F32) for s in range(NX)])
            Ah[:, pl.ds(h * HD, HD)] = o.astype(BF)

        @pl.when(c == 1)
        def _():
            put(Ah, att.at[:, pl.ds(512, 512)], 22, sib)

        @pl.when(c == 0)
        def _():
            att[:, pl.ds(0, 512)] = Ah[...]
            wait_for(Ah, rsem.at[22])

    wait_for(Gr.at[pl.ds(0, 15)], rsem.at[14])
    grad[...] = functools.reduce(jnp.add, [Gr[s].astype(F32) for s in range(16)])

    @pl.when(main)
    def _():
        wait_for(Kx.at[pl.ds(0, 7)], ssem.at[0])
        wait_for(Kx, ssem.at[16])
        wait_for(Qpos, ssem.at[3])
        wait_for(Qb.at[0], ssem.at[19])
        wait_for(Cb.at[0], ssem.at[20])
        wait_for(Vb.at[pl.ds(0, 7 * TOK), :], ssem.at[11])
        wait_for(Vb, ssem.at[18])

    @pl.when(side)
    def _():
        wait_for(Ah, ssem.at[22])

    @pl.when(half_owner)
    def _():
        wait_for(Vg.at[pl.ds(0, 7)], ssem.at[4])

    wait_for(Wg.at[pl.ds(0, 3)], ssem.at[17])
    wait_for(Hf.at[0], ssem.at[21])
    wait_for(Hs.at[pl.ds(0, 7)], ssem.at[5])
    wait_for(Vp, ssem.at[8])

    @pl.when(trace)
    def _():
        wait_for(Qb.at[pl.ds(0, 3)], ssem.at[2])
        wait_for(Cb.at[pl.ds(0, 3)], ssem.at[6])
        wait_for(ML.at[pl.ds(0, 3)], ssem.at[7])
        wait_for(Tsend, ssem.at[9])
        wait_for(Or.at[pl.ds(0, 3)], ssem.at[15])

    @pl.when(trace_owner)
    def _():
        wait_for(Tz.at[pl.ds(0, 3)], ssem.at[10])

    @pl.when(jnp.logical_and(trace, jnp.logical_not(trace_owner)))
    def _():
        wait_for(Tz, ssem.at[10])

    @pl.when(owner)
    def _():
        wait_for(Vg.at[pl.ds(0, 7)], ssem.at[12])

    @pl.when(c == 1)
    def _():
        wait_for(Vg.at[pl.ds(0, 7)], ssem.at[13])

    wait_for(Gr.at[pl.ds(0, 15)], ssem.at[14])


def per_device(hidden_in, value_weight, queries, key_vectors, cotangent, doc_ids, positions):
    vmem = pl.BlockSpec(memory_space=pltpu.VMEM)
    hbm = pl.BlockSpec(memory_space=pltpu.HBM)
    scratch = [
        pltpu.VMEM((1, TOK), jnp.int32),
        pltpu.VMEM((1, TOK), jnp.int32),
        pltpu.VMEM((8, TOK), jnp.int32),
        pltpu.VMEM((TOK + 16, HD), BF),
        pltpu.VMEM((NX, 512, HD), BF),
        pltpu.VMEM((2, TOK, 2048), BF),
        pltpu.VMEM((8, TOK, 512), BF),
        pltpu.VMEM((512, 1024), BF),
        pltpu.VMEM((NZ, TOK + 16, HD), BF),
        pltpu.VMEM((1024, TOK), F32),
        pltpu.VMEM((NX, TOK, 512), BF),
        pltpu.VMEM((7, 8, TOK), jnp.int32),
        pltpu.VMEM((NX, TOK, 512), BF),
        pltpu.VMEM((TOK, 1024), BF),
        pltpu.VMEM((TOK, 1024), BF),
        pltpu.VMEM((1024, 256), F32),
        pltpu.VMEM((1024, 2048), BF),
        pltpu.VMEM((NX, NX, 8, 256), F32),
        pltpu.VMEM((NX, 8, 256), F32),
        pltpu.VMEM((2048, HD), BF),
        pltpu.VMEM((TOK, HD), F32),
        pltpu.VMEM((TOK, HD), F32),
        pltpu.VMEM((1024, HD), BF),
        pltpu.VMEM((HD, 1024), BF),
        pltpu.VMEM((512, HD), BF),
        pltpu.VMEM((512, HD), BF),
        pltpu.VMEM((4, TOK, HD), BF),
        pltpu.VMEM((8, TOK, HD), BF),
        pltpu.VMEM((8, TOK, HD), BF),
        pltpu.VMEM((NX, 512, HD), BF),
        pltpu.VMEM((NX, 512, HD), BF),
        pltpu.VMEM((TOK, 512), BF),
        pltpu.VMEM((16, 32, HD), BF),
        pltpu.VMEM((16, 32, HD), BF),
        pltpu.SemaphoreType.DMA((23,)),
        pltpu.SemaphoreType.DMA((23,)),
        pltpu.SemaphoreType.DMA((9,)),
        pltpu.SemaphoreType.REGULAR,
    ]
    return pl.pallas_call(
        kernel,
        name="trace_attention",
        out_shape=(
            jax.ShapeDtypeStruct((TOK, 1024), BF),
            jax.ShapeDtypeStruct((32, HD), F32),
        ),
        in_specs=[hbm] * 7,
        out_specs=(vmem, vmem),
        scratch_shapes=scratch,
        compiler_params=pltpu.CompilerParams(
            collective_id=0, has_side_effects=True, vmem_limit_bytes=56 << 20
        ),
    )(
        hidden_in, value_weight, queries, key_vectors, cotangent,
        doc_ids.reshape(1, TOK), positions.reshape(1, TOK),
    )


def solution(mesh):
    in_specs = (
        P(("grp", "blk"), None),
        P("blk", "tp"),
        P(("grp", "blk"), "tp"),
        P(("grp", "blk"), "tp"),
        P(("grp", "blk"), "tp"),
        P(("grp", "blk")),
        P(("grp", "blk")),
    )
    out_specs = (P(("grp", "blk"), "tp"), P(("grp", "blk"), "tp"))
    return jax.shard_map(
        per_device, mesh=mesh, in_specs=in_specs, out_specs=out_specs, check_vma=False
    )
```

```python
import functools
import math

import jax
import jax.numpy as jnp
from jax import lax
from jax.experimental import pallas as pl
from jax.experimental.pallas import tpu as pltpu
from jax.sharding import PartitionSpec as P

HD = 128
NX = 4
NZ = 8
TOK = 128
SCALE = HD ** (-0.5) * math.log2(math.e)
HIDDEN = -1e30
MESH = pl.DeviceIdType.MESH
BF = jnp.bfloat16
F32 = jnp.float32
NT = (((1,), (1,)), ((), ()))


def wait_for(ref, sem):
    pltpu.make_async_copy(ref, ref, sem).wait()


def flip(row, rows):
    return jnp.transpose(jnp.broadcast_to(row, (rows, row.shape[1])))


def stack_pair(block):
    return jnp.concatenate([block[:, :HD], block[:, HD:]], axis=0)


def kernel(
    hid, wgt, qry, key, cot, doc, pos,
    att, grad,
    posv, docv, posb, Kv, Wg, Hf, Hs, HsT, Kx, KposT, Qb, Qpos, Cb, Qf, Cf, Sb, Pm, ML, Wr, Cs,
    Vp, Vs, Vb, VT, Tsend, Tsib, Tz, Tr, Vg, Ost, Or, Ah, Gst, Gr,
    ssem, rsem, lsem, far_in,
):
    grp = lax.axis_index("grp")
    blk = lax.axis_index("blk")
    tp = lax.axis_index("tp")
    zh, c = grp // 2, grp % 2
    x, z = blk // NZ, blk % NZ
    me = x * 2 + c
    z16 = zh * NZ + z
    trace = zh == 0
    main = jnp.logical_and(trace, c == 0)
    side = jnp.logical_and(trace, c == 1)
    local = jnp.logical_not(main)
    half_owner = z // 4 == c
    owner = jnp.where(trace, half_owner, c == 0)
    trace_owner = jnp.logical_and(trace, half_owner)

    def dev(x_, z_, zh_, c_):
        return (zh_ * 2 + c_, x_ * NZ + z_, tp)

    def put(src, dst, phase, to):
        pltpu.make_async_remote_copy(
            src_ref=src, dst_ref=dst, send_sem=ssem.at[phase], recv_sem=rsem.at[phase],
            device_id=to, device_id_type=MESH,
        ).start()

    near = []
    for k in (1, 2, 7, 6, 3, 5, 4):
        s = (me + k) % 8
        near.append((s // 2, s % 2))
    sib = dev(x, z, zh, 1 - c)
    line = [(z + k) % NZ for k in (4, 3, 5, 2, 6, 1, 7)]
    ring = [(x + k) % NX for k in (2, 1, 3)]
    half = pl.multiple_of(c * 512, 512)

    bar = pltpu.get_barrier_semaphore()

    def greet(to):
        pl.semaphore_signal(bar, inc=1, device_id=to, device_id_type=MESH)

    for xs, cs in near:
        greet(dev(xs, z, zh, cs))
    for zz in line:
        greet(dev(x, zz, zh, c))

    @pl.when(trace)
    def _():
        for zz in range(NZ):
            greet(dev(x, zz, 1, c))

    pltpu.make_async_copy(key, Kv.at[pl.ds(0, TOK), :], lsem.at[6]).start()
    pltpu.make_async_copy(pos, posv, lsem.at[7]).start()
    pltpu.make_async_copy(doc, docv, lsem.at[8]).start()
    for k in range(NX):
        pltpu.make_async_copy(
            hid.at[:, pl.ds(pl.multiple_of(k * 1024 + half, 512), 512)],
            Hf.at[c, :, pl.ds(k * 512, 512)], lsem.at[0]).start()
    for gi in range(2):
        pltpu.make_async_copy(
            hid.at[:, pl.ds(pl.multiple_of((c + 2 * gi) * 1024 + x * 256, 256), 256)],
            Hs.at[me, :, pl.ds(gi * 256, 256)], lsem.at[1]).start()

    @pl.when(main)
    def _():
        pltpu.make_async_copy(qry.at[:, pl.ds(0, 512)], Qb.at[x], lsem.at[2]).start()
        pltpu.make_async_copy(cot.at[:, pl.ds(0, 512)], Cb.at[x], lsem.at[3]).start()

    @pl.when(local)
    def _():
        pltpu.make_async_copy(qry, Qf, lsem.at[4]).start()
        pltpu.make_async_copy(cot, Cf, lsem.at[5]).start()

    wait_for(Kv.at[pl.ds(0, TOK), :], lsem.at[6])
    wait_for(posv, lsem.at[7])
    wait_for(docv, lsem.at[8])
    posb[...] = jnp.broadcast_to(posv[...], (8, TOK))
    p_row = posv[...].astype(F32)
    p_high = jnp.floor(p_row * (1.0 / 64.0))
    Kv[pl.ds(TOK, 16), :] = jnp.concatenate(
        [jnp.broadcast_to(p_high, (8, TOK)), jnp.broadcast_to(p_row - 64.0 * p_high, (8, TOK))],
        axis=0).astype(BF)

    @pl.when(main)
    def _():
        Kx[z] = Kv[...]
        Qpos[x] = posb[...]

    pl.semaphore_wait(bar, jnp.where(trace, 14, 22))

    slot = pl.ds(pl.multiple_of((z % 4) * TOK, TOK), TOK)

    @pl.when(half_owner)
    def _():
        pltpu.make_async_copy(wgt, Wg.at[x, slot, :], rsem.at[4]).start()
        for zz in line:
            put(wgt, Wg.at[x, slot, :], 4, dev(x, zz, zh, c))

    @pl.when(main)
    def _():
        put(qry.at[:, pl.ds(512, 512)], Qb.at[x], 19, sib)
        for zz in line:
            put(Kv, Kx.at[z], 0, dev(x, zz, zh, 0))
        for xt in ring:
            put(qry.at[:, pl.ds(0, 512)], Qb.at[x], 2, dev(xt, z, zh, 0))
        for xs, cs in near:
            put(posb, Qpos.at[x], 3, dev(xs, z, zh, cs))
        put(cot.at[:, pl.ds(512, 512)], Cb.at[x], 20, sib)

    @pl.when(main)
    def _():
        for xt in ring:
            put(cot.at[:, pl.ds(0, 512)], Cb.at[x], 6, dev(xt, z, zh, 0))

    for k in range(NX):
        put(hid.at[:, pl.ds(pl.multiple_of(k * 1024 + (1 - c) * 512, 512), 512)],
            Hf.at[c, :, pl.ds(k * 512, 512)], 21, sib)

    @pl.when(zh != 0)
    def _():
        for zz in range(NZ):
            pl.semaphore_signal(
                far_in, inc=1, device_id=dev(x, zz, 0, c), device_id_type=MESH)

    @pl.when(side)
    def _():
        wait_for(Qb.at[0], rsem.at[19])
        for xt in ring:
            put(Qb.at[x], Qb.at[x], 2, dev(xt, z, zh, 1))
        wait_for(Cb.at[0], rsem.at[20])
        for xt in ring:
            put(Cb.at[x], Cb.at[x], 6, dev(xt, z, zh, 1))

    @pl.when(main)
    def _():
        wait_for(Kx.at[pl.ds(0, 7)], rsem.at[0])
        put(Kx, Kx, 16, sib)

    wait_for(Wg.at[0], rsem.at[4])
    for xt in ring:
        put(Wg.at[x], Wg.at[x], 17, dev(xt, z, zh, c))

    @pl.when(trace)
    def _():
        @pl.when(c == 0)
        def _():
            wait_for(Qpos.at[pl.ds(0, 3)], rsem.at[3])
            wait_for(Qb.at[0], lsem.at[2])

        @pl.when(c == 1)
        def _():
            wait_for(Kx, rsem.at[16])
            wait_for(Qpos.at[pl.ds(0, 4)], rsem.at[3])

        wait_for(Qb.at[pl.ds(0, 3)], rsem.at[2])

        for t in range(NZ):
            digits = Kx[t, pl.ds(TOK, 16), :].astype(F32)
            KposT[pl.ds(t * TOK, TOK), :] = flip(digits[0:1] * 64.0 + digits[8:9], TOK)

        def score_block(xq, carry):
            q_at = Qpos[xq][0:1, :].astype(F32)
            tops, sums = [], []
            for pair in range(2):
                qp = stack_pair(Qb[xq, :, pl.ds(pair * 256, 256)])
                top = jnp.full((8, 256), HIDDEN, F32)
                for t in range(4):
                    rows = pl.ds(t * 256, 256)
                    kk = jnp.concatenate(
                        [Kx[2 * t, pl.ds(0, TOK), :], Kx[2 * t + 1, pl.ds(0, TOK), :]], axis=0)
                    s = lax.dot_general(kk, qp, NT, preferred_element_type=F32)
                    seen = KposT[rows, :] <= q_at
                    s = jnp.concatenate(
                        [jnp.where(seen, s[:, :HD], HIDDEN), jnp.where(seen, s[:, HD:], HIDDEN)],
                        axis=1)
                    Sb[rows, :] = s
                    top = jnp.maximum(top, jnp.max(s.reshape(32, 8, 256), axis=0))
                m = jnp.max(top, axis=0, keepdims=True) * SCALE
                total = jnp.zeros((8, 256), F32)
                at = pl.ds(pl.multiple_of(xq * 512 + pair * 256, 256), 256)
                for t in range(8):
                    rows = pl.ds(t * TOK, TOK)
                    p = jnp.exp2(Sb[rows, :] * SCALE - m)
                    total = total + jnp.sum(p.reshape(16, 8, 256), axis=0)
                    Pm[rows, at] = p.astype(BF)
                tops.append(m)
                sums.append(jnp.sum(total, axis=0, keepdims=True))
            ML[x, xq] = jnp.concatenate(
                tops + sums + [jnp.zeros((4, 256), F32)], axis=0)
            return carry

        lax.fori_loop(0, NX, score_block, 0)
        for xt in ring:
            put(ML.at[x], ML.at[x], 7, dev(xt, z, zh, c))

    for xs, cs in near:
        for gi in range(2):
            col = pl.multiple_of((cs + 2 * gi) * 1024 + xs * 256, 256)
            put(hid.at[:, pl.ds(col, 256)], Hs.at[me, :, pl.ds(gi * 256, 256)], 5,
                dev(xs, z, zh, cs))

    wait_for(Wg.at[pl.ds(0, 3)], rsem.at[17])
    wait_for(Hf.at[0], lsem.at[0])
    wait_for(Hf.at[0], rsem.at[21])
    w_all = Wg[...].reshape(2048, HD)
    Vp[...] = jnp.dot(Hf[1 - c], w_all, preferred_element_type=F32)
    put(Vp, Vs, 8, sib)
    own_part = jnp.dot(Hf[c], w_all, preferred_element_type=F32)
    wait_for(Vs, rsem.at[8])
    val = (own_part + Vs[...]).astype(BF)

    @pl.when(main)
    def _():
        rows = pl.ds(pl.multiple_of(z * TOK, TOK), TOK)
        Vb[rows, :] = val
        for zz in line:
            put(Vb.at[rows, :], Vb.at[rows, :], 11, dev(x, zz, zh, 0))

    @pl.when(trace)
    def _():
        @pl.when(c == 0)
        def _():
            wait_for(Cb.at[0], lsem.at[3])

        wait_for(Cb.at[pl.ds(0, 3)], rsem.at[6])
        wait_for(ML.at[pl.ds(0, 3)], rsem.at[7])

        def scale_block(xq, carry):
            parts = [ML[s, xq] for s in range(NX)]
            high = functools.reduce(jnp.maximum, [p[0:2] for p in parts])
            total = functools.reduce(
                jnp.add, [p[2:4] * jnp.exp2(p[0:2] - high) for p in parts])
            w = jnp.exp2(ML[x, xq][0:2] - high) / total
            Wr[xq] = jnp.concatenate([w, jnp.zeros((6, 256), F32)], axis=0)
            for pair in range(2):
                cp = stack_pair(Cb[xq, :, pl.ds(pair * 256, 256)]).astype(F32)
                rows = pl.ds(pl.multiple_of(xq * 512 + pair * 256, 256), 256)
                Cs[rows, :] = (cp * flip(w[pair:pair + 1], TOK)).astype(BF)
            return carry

        lax.fori_loop(0, NX, scale_block, 0)
        theirs = pl.ds(pl.multiple_of((1 - c) * 512, 512), 512)
        ours = pl.ds(half, 512)
        Tsend[...] = jnp.dot(Pm[theirs, :], Cs[...], preferred_element_type=F32).astype(BF)
        put(Tsend, Tsib, 9, sib)
        mine = jnp.dot(Pm[ours, :], Cs[...], preferred_element_type=F32)
        wait_for(Tsib, rsem.at[9])
        Tz[...] = (mine + Tsib[...].astype(F32)).astype(BF).reshape(4, TOK, HD)
        for k in range(4):
            zt = 4 * c + k

            @pl.when(zt != z)
            def _():
                put(Tz.at[k], Tr.at[z], 10, dev(x, zt, zh, c))

            @pl.when(zt == z)
            def _():
                Tr[z] = Tz[k]

    @pl.when(local)
    def _():
        wait_for(Qf, lsem.at[4])
        wait_for(Cf, lsem.at[5])
        val_t = jnp.transpose(val)
        d_row = docv[...].astype(F32)
        seen = jnp.logical_and(flip(p_row, TOK) <= p_row, flip(d_row, TOK) == d_row)
        terms = jnp.zeros((TOK, HD), F32)
        for pair in range(4):
            qp = stack_pair(Qf[:, pl.ds(pair * 256, 256)])
            s = lax.dot_general(Kv[pl.ds(0, TOK), :], qp, NT, preferred_element_type=F32)
            s = jnp.concatenate(
                [jnp.where(seen, s[:, :HD], HIDDEN), jnp.where(seen, s[:, HD:], HIDDEN)], axis=1)
            s = s * SCALE
            p = jnp.exp2(s - jnp.max(s, axis=0, keepdims=True))
            w = 1.0 / jnp.sum(p, axis=0, keepdims=True)
            pb = (p * w).astype(BF)
            o = jnp.dot(val_t, pb, preferred_element_type=F32)
            att[:, pl.ds(pair * 256, HD)] = jnp.transpose(o[:, :HD]).astype(BF)
            att[:, pl.ds(pair * 256 + HD, HD)] = jnp.transpose(o[:, HD:]).astype(BF)
            cp = stack_pair(Cf[:, pl.ds(pair * 256, 256)])
            terms = terms + jnp.dot(pb, cp, preferred_element_type=F32)
        Vg[me] = terms.astype(BF)
        for phase, core in ((12, 0), (13, 1)):
            @pl.when(c == core)
            def _():
                for xs, cs in near:
                    put(Vg.at[me], Vg.at[me], phase, dev(xs, z, zh, cs))

    wait_for(Hs.at[pl.ds(0, 7)], rsem.at[5])
    wait_for(Hs.at[0], lsem.at[1])
    for s in range(8):
        HsT[:, pl.ds(s * TOK, TOK)] = jnp.transpose(Hs[s])

    @pl.when(main)
    def _():
        wait_for(Vb.at[pl.ds(0, 7 * TOK), :], rsem.at[11])
        put(Vb, Vb, 18, sib)

    @pl.when(trace_owner)
    def _():
        wait_for(Tr.at[pl.ds(0, 7)], rsem.at[10])
        Vg[2 * x] = functools.reduce(
            jnp.add, [Tr[s].astype(F32) for s in range(NZ)]).astype(BF)
        for xs, cs in near:
            put(Vg.at[2 * x], Vg.at[2 * x], 12, dev(xs, z, zh, cs))

    @pl.when(trace)
    def _():
        @pl.when(c == 1)
        def _():
            wait_for(Vb, rsem.at[18])

        VT[...] = jnp.transpose(Vb[...])

        def out_block(xq, carry):
            w = Wr[xq]
            for pair in range(2):
                at = pl.ds(pl.multiple_of(xq * 512 + pair * 256, 256), 256)
                o = jnp.dot(VT[...], Pm[:, at], preferred_element_type=F32) * w[pair:pair + 1]
                Ost[xq, pl.ds(pair * 256, 256), :] = jnp.transpose(o).astype(BF)
            return carry

        lax.fori_loop(0, NX, out_block, 0)
        for xt in ring:
            put(Ost.at[xt], Or.at[x], 15, dev(xt, z, zh, c))
        Or[x] = Ost[x]

    for phase, sender in ((12, owner), (13, c == 1)):
        @pl.when(sender)
        def _():
            wait_for(Vg.at[pl.ds(0, 3)], rsem.at[phase])

        @pl.when(jnp.logical_not(sender))
        def _():
            wait_for(Vg.at[pl.ds(0, 4)], rsem.at[phase])

    vg_all = Vg[...].reshape(8 * TOK, HD)
    Gst[...] = jnp.dot(HsT[...], vg_all, preferred_element_type=F32).astype(BF).reshape(16, 32, HD)

    @pl.when(trace)
    def _():
        pl.semaphore_wait(far_in, NZ)

    for k in (8, 7, 9, 6, 10, 5, 11, 4, 12, 3, 13, 2, 14, 1, 15):
        zz = (z16 + k) % 16
        put(Gst.at[zz], Gr.at[z16], 14, dev(x, zz % NZ, zz // NZ, c))
    Gr[z16] = Gst[z16]

    @pl.when(trace)
    def _():
        wait_for(Or.at[pl.ds(0, 3)], rsem.at[15])
        for h in range(4):
            o = functools.reduce(
                jnp.add, [Or[s, pl.ds(h * TOK, TOK), :].astype(F32) for s in range(NX)])
            Ah[:, pl.ds(h * HD, HD)] = o.astype(BF)

        @pl.when(c == 1)
        def _():
            put(Ah, att.at[:, pl.ds(512, 512)], 22, sib)

        @pl.when(c == 0)
        def _():
            att[:, pl.ds(0, 512)] = Ah[...]
            wait_for(Ah, rsem.at[22])

    wait_for(Gr.at[pl.ds(0, 15)], rsem.at[14])
    grad[...] = functools.reduce(jnp.add, [Gr[s].astype(F32) for s in range(16)])

    @pl.when(main)
    def _():
        wait_for(Kx.at[pl.ds(0, 7)], ssem.at[0])
        wait_for(Kx, ssem.at[16])
        wait_for(Qpos, ssem.at[3])
        wait_for(Qb.at[0], ssem.at[19])
        wait_for(Cb.at[0], ssem.at[20])
        wait_for(Vb.at[pl.ds(0, 7 * TOK), :], ssem.at[11])
        wait_for(Vb, ssem.at[18])

    @pl.when(side)
    def _():
        wait_for(Ah, ssem.at[22])

    @pl.when(half_owner)
    def _():
        wait_for(Vg.at[pl.ds(0, 7)], ssem.at[4])

    wait_for(Wg.at[pl.ds(0, 3)], ssem.at[17])
    wait_for(Hf.at[0], ssem.at[21])
    wait_for(Hs.at[pl.ds(0, 7)], ssem.at[5])
    wait_for(Vp, ssem.at[8])

    @pl.when(trace)
    def _():
        wait_for(Qb.at[pl.ds(0, 3)], ssem.at[2])
        wait_for(Cb.at[pl.ds(0, 3)], ssem.at[6])
        wait_for(ML.at[pl.ds(0, 3)], ssem.at[7])
        wait_for(Tsend, ssem.at[9])
        wait_for(Or.at[pl.ds(0, 3)], ssem.at[15])

    @pl.when(trace_owner)
    def _():
        wait_for(Tz.at[pl.ds(0, 3)], ssem.at[10])

    @pl.when(jnp.logical_and(trace, jnp.logical_not(trace_owner)))
    def _():
        wait_for(Tz, ssem.at[10])

    @pl.when(owner)
    def _():
        wait_for(Vg.at[pl.ds(0, 7)], ssem.at[12])

    @pl.when(c == 1)
    def _():
        wait_for(Vg.at[pl.ds(0, 7)], ssem.at[13])

    wait_for(Gr.at[pl.ds(0, 15)], ssem.at[14])


def per_device(hidden_in, value_weight, queries, key_vectors, cotangent, doc_ids, positions):
    vmem = pl.BlockSpec(memory_space=pltpu.VMEM)
    hbm = pl.BlockSpec(memory_space=pltpu.HBM)
    scratch = [
        pltpu.VMEM((1, TOK), jnp.int32),
        pltpu.VMEM((1, TOK), jnp.int32),
        pltpu.VMEM((8, TOK), jnp.int32),
        pltpu.VMEM((TOK + 16, HD), BF),
        pltpu.VMEM((NX, 512, HD), BF),
        pltpu.VMEM((2, TOK, 2048), BF),
        pltpu.VMEM((8, TOK, 512), BF),
        pltpu.VMEM((512, 1024), BF),
        pltpu.VMEM((NZ, TOK + 16, HD), BF),
        pltpu.VMEM((1024, TOK), F32),
        pltpu.VMEM((NX, TOK, 512), BF),
        pltpu.VMEM((7, 8, TOK), jnp.int32),
        pltpu.VMEM((NX, TOK, 512), BF),
        pltpu.VMEM((TOK, 1024), BF),
        pltpu.VMEM((TOK, 1024), BF),
        pltpu.VMEM((1024, 256), F32),
        pltpu.VMEM((1024, 2048), BF),
        pltpu.VMEM((NX, NX, 8, 256), F32),
        pltpu.VMEM((NX, 8, 256), F32),
        pltpu.VMEM((2048, HD), BF),
        pltpu.VMEM((TOK, HD), F32),
        pltpu.VMEM((TOK, HD), F32),
        pltpu.VMEM((1024, HD), BF),
        pltpu.VMEM((HD, 1024), BF),
        pltpu.VMEM((512, HD), BF),
        pltpu.VMEM((512, HD), BF),
        pltpu.VMEM((4, TOK, HD), BF),
        pltpu.VMEM((8, TOK, HD), BF),
        pltpu.VMEM((8, TOK, HD), BF),
        pltpu.VMEM((NX, 512, HD), BF),
        pltpu.VMEM((NX, 512, HD), BF),
        pltpu.VMEM((TOK, 512), BF),
        pltpu.VMEM((16, 32, HD), BF),
        pltpu.VMEM((16, 32, HD), BF),
        pltpu.SemaphoreType.DMA((23,)),
        pltpu.SemaphoreType.DMA((23,)),
        pltpu.SemaphoreType.DMA((9,)),
        pltpu.SemaphoreType.REGULAR,
    ]
    return pl.pallas_call(
        kernel,
        name="trace_attention",
        out_shape=(
            jax.ShapeDtypeStruct((TOK, 1024), BF),
            jax.ShapeDtypeStruct((32, HD), F32),
        ),
        in_specs=[hbm] * 7,
        out_specs=(vmem, vmem),
        scratch_shapes=scratch,
        compiler_params=pltpu.CompilerParams(
            collective_id=0, has_side_effects=True, vmem_limit_bytes=56 << 20
        ),
    )(
        hidden_in, value_weight, queries, key_vectors, cotangent,
        doc_ids.reshape(1, TOK), positions.reshape(1, TOK),
    )


def solution(mesh):
    in_specs = (
        P(("grp", "blk"), None),
        P("blk", "tp"),
        P(("grp", "blk"), "tp"),
        P(("grp", "blk"), "tp"),
        P(("grp", "blk"), "tp"),
        P(("grp", "blk")),
        P(("grp", "blk")),
    )
    out_specs = (P(("grp", "blk"), "tp"), P(("grp", "blk"), "tp"))
    return jax.shard_map(
        per_device, mesh=mesh, in_specs=in_specs, out_specs=out_specs, check_vma=False
    )
```

```python
import functools
import math

import jax
import jax.numpy as jnp
from jax import lax
from jax.experimental import pallas as pl
from jax.experimental.pallas import tpu as pltpu
from jax.sharding import PartitionSpec as P

HD = 128
NX = 4
NZ = 8
TOK = 128
SCALE = HD ** (-0.5) * math.log2(math.e)
HIDDEN = -1e30
MESH = pl.DeviceIdType.MESH
BF = jnp.bfloat16
F32 = jnp.float32
NT = (((1,), (1,)), ((), ()))


def wait_for(ref, sem):
    pltpu.make_async_copy(ref, ref, sem).wait()


def flip(row, rows):
    return jnp.transpose(jnp.broadcast_to(row, (rows, row.shape[1])))


def stack_pair(block):
    return jnp.concatenate([block[:, :HD], block[:, HD:]], axis=0)


def kernel(
    hid, wgt, qry, key, cot, doc, pos,
    att, grad,
    posv, docv, posb, Kv, Wg, Hf, Hs, HsT, Kx, KposT, Qb, Qpos, Cb, Qf, Cf, Sb, Pm, ML, Wr, Cs,
    Vp, Vs, Vb, VT, Tsend, Tsib, Tz, Tr, Vg, Ost, Or, Ah, Gst, Gr,
    ssem, rsem, lsem, far_in,
):
    grp = lax.axis_index("grp")
    blk = lax.axis_index("blk")
    tp = lax.axis_index("tp")
    zh, c = grp // 2, grp % 2
    x, z = blk // NZ, blk % NZ
    me = x * 2 + c
    z16 = zh * NZ + z
    trace = zh == 0
    main = jnp.logical_and(trace, c == 0)
    side = jnp.logical_and(trace, c == 1)
    local = jnp.logical_not(main)
    half_owner = z // 4 == c
    owner = jnp.where(trace, half_owner, c == 0)
    trace_owner = jnp.logical_and(trace, half_owner)

    def dev(x_, z_, zh_, c_):
        return (zh_ * 2 + c_, x_ * NZ + z_, tp)

    def put(src, dst, phase, to):
        pltpu.make_async_remote_copy(
            src_ref=src, dst_ref=dst, send_sem=ssem.at[phase], recv_sem=rsem.at[phase],
            device_id=to, device_id_type=MESH,
        ).start()

    near = []
    for k in (1, 2, 7, 6, 3, 5, 4):
        s = (me + k) % 8
        near.append((s // 2, s % 2))
    sib = dev(x, z, zh, 1 - c)
    line = [(z + k) % NZ for k in (4, 3, 5, 2, 6, 1, 7)]
    ring = [(x + k) % NX for k in (2, 1, 3)]
    half = pl.multiple_of(c * 512, 512)

    bar = pltpu.get_barrier_semaphore()

    def greet(to):
        pl.semaphore_signal(bar, inc=1, device_id=to, device_id_type=MESH)

    for xs, cs in near:
        greet(dev(xs, z, zh, cs))
    for zz in line:
        greet(dev(x, zz, zh, c))

    @pl.when(trace)
    def _():
        for zz in range(NZ):
            greet(dev(x, zz, 1, c))

    pltpu.make_async_copy(key, Kv.at[pl.ds(0, TOK), :], lsem.at[6]).start()
    pltpu.make_async_copy(pos, posv, lsem.at[7]).start()
    pltpu.make_async_copy(doc, docv, lsem.at[8]).start()
    for k in range(NX):
        pltpu.make_async_copy(
            hid.at[:, pl.ds(pl.multiple_of(k * 1024 + half, 512), 512)],
            Hf.at[c, :, pl.ds(k * 512, 512)], lsem.at[0]).start()
    for gi in range(2):
        pltpu.make_async_copy(
            hid.at[:, pl.ds(pl.multiple_of((c + 2 * gi) * 1024 + x * 256, 256), 256)],
            Hs.at[me, :, pl.ds(gi * 256, 256)], lsem.at[1]).start()

    @pl.when(main)
    def _():
        pltpu.make_async_copy(qry.at[:, pl.ds(0, 512)], Qb.at[x], lsem.at[2]).start()
        pltpu.make_async_copy(cot.at[:, pl.ds(0, 512)], Cb.at[x], lsem.at[3]).start()

    @pl.when(local)
    def _():
        pltpu.make_async_copy(qry, Qf, lsem.at[4]).start()
        pltpu.make_async_copy(cot, Cf, lsem.at[5]).start()

    wait_for(Kv.at[pl.ds(0, TOK), :], lsem.at[6])
    wait_for(posv, lsem.at[7])
    wait_for(docv, lsem.at[8])
    posb[...] = jnp.broadcast_to(posv[...], (8, TOK))
    p_row = posv[...].astype(F32)
    p_high = jnp.floor(p_row * (1.0 / 64.0))
    Kv[pl.ds(TOK, 16), :] = jnp.concatenate(
        [jnp.broadcast_to(p_high, (8, TOK)), jnp.broadcast_to(p_row - 64.0 * p_high, (8, TOK))],
        axis=0).astype(BF)

    @pl.when(main)
    def _():
        Kx[z] = Kv[...]
        Qpos[x] = posb[...]

    pl.semaphore_wait(bar, jnp.where(trace, 14, 22))

    slot = pl.ds(pl.multiple_of((z % 4) * TOK, TOK), TOK)

    @pl.when(half_owner)
    def _():
        pltpu.make_async_copy(wgt, Wg.at[x, slot, :], rsem.at[4]).start()
        for zz in line:
            put(wgt, Wg.at[x, slot, :], 4, dev(x, zz, zh, c))

    @pl.when(main)
    def _():
        put(qry.at[:, pl.ds(512, 512)], Qb.at[x], 19, sib)
        for zz in line:
            put(Kv, Kx.at[z], 0, dev(x, zz, zh, 0))
        for xt in ring:
            put(qry.at[:, pl.ds(0, 512)], Qb.at[x], 2, dev(xt, z, zh, 0))
        for xs, cs in near:
            put(posb, Qpos.at[x], 3, dev(xs, z, zh, cs))
        put(cot.at[:, pl.ds(512, 512)], Cb.at[x], 20, sib)

    @pl.when(main)
    def _():
        for xt in ring:
            put(cot.at[:, pl.ds(0, 512)], Cb.at[x], 6, dev(xt, z, zh, 0))

    for k in range(NX):
        put(hid.at[:, pl.ds(pl.multiple_of(k * 1024 + (1 - c) * 512, 512), 512)],
            Hf.at[c, :, pl.ds(k * 512, 512)], 21, sib)

    @pl.when(zh != 0)
    def _():
        for zz in range(NZ):
            pl.semaphore_signal(
                far_in, inc=1, device_id=dev(x, zz, 0, c), device_id_type=MESH)

    @pl.when(side)
    def _():
        wait_for(Qb.at[0], rsem.at[19])
        for xt in ring:
            put(Qb.at[x], Qb.at[x], 2, dev(xt, z, zh, 1))
        wait_for(Cb.at[0], rsem.at[20])
        for xt in ring:
            put(Cb.at[x], Cb.at[x], 6, dev(xt, z, zh, 1))

    @pl.when(main)
    def _():
        wait_for(Kx.at[pl.ds(0, 7)], rsem.at[0])
        put(Kx, Kx, 16, sib)

    wait_for(Wg.at[0], rsem.at[4])
    for xt in ring:
        put(Wg.at[x], Wg.at[x], 17, dev(xt, z, zh, c))

    @pl.when(trace)
    def _():
        @pl.when(c == 0)
        def _():
            wait_for(Qpos.at[pl.ds(0, 3)], rsem.at[3])
            wait_for(Qb.at[0], lsem.at[2])

        @pl.when(c == 1)
        def _():
            wait_for(Kx, rsem.at[16])
            wait_for(Qpos.at[pl.ds(0, 4)], rsem.at[3])

        wait_for(Qb.at[pl.ds(0, 3)], rsem.at[2])

        for t in range(NZ):
            digits = Kx[t, pl.ds(TOK, 16), :].astype(F32)
            KposT[pl.ds(t * TOK, TOK), :] = flip(digits[0:1] * 64.0 + digits[8:9], TOK)

        def score_block(xq, carry):
            q_at = Qpos[xq][0:1, :].astype(F32)
            tops, sums = [], []
            for pair in range(2):
                qp = stack_pair(Qb[xq, :, pl.ds(pair * 256, 256)])
                top = jnp.full((8, 256), HIDDEN, F32)
                for t in range(4):
                    rows = pl.ds(t * 256, 256)
                    kk = jnp.concatenate(
                        [Kx[2 * t, pl.ds(0, TOK), :], Kx[2 * t + 1, pl.ds(0, TOK), :]], axis=0)
                    s = lax.dot_general(kk, qp, NT, preferred_element_type=F32)
                    seen = KposT[rows, :] <= q_at
                    s = jnp.concatenate(
                        [jnp.where(seen, s[:, :HD], HIDDEN), jnp.where(seen, s[:, HD:], HIDDEN)],
                        axis=1)
                    Sb[rows, :] = s
                    top = jnp.maximum(top, jnp.max(s.reshape(32, 8, 256), axis=0))
                m = jnp.max(top, axis=0, keepdims=True) * SCALE
                total = jnp.zeros((8, 256), F32)
                at = pl.ds(pl.multiple_of(xq * 512 + pair * 256, 256), 256)
                for t in range(8):
                    rows = pl.ds(t * TOK, TOK)
                    p = jnp.exp2(Sb[rows, :] * SCALE - m)
                    total = total + jnp.sum(p.reshape(16, 8, 256), axis=0)
                    Pm[rows, at] = p.astype(BF)
                tops.append(m)
                sums.append(jnp.sum(total, axis=0, keepdims=True))
            ML[x, xq] = jnp.concatenate(
                tops + sums + [jnp.zeros((4, 256), F32)], axis=0)
            return carry

        lax.fori_loop(0, NX, score_block, 0)
        for xt in ring:
            put(ML.at[x], ML.at[x], 7, dev(xt, z, zh, c))

    for xs, cs in near:
        for gi in range(2):
            col = pl.multiple_of((cs + 2 * gi) * 1024 + xs * 256, 256)
            put(hid.at[:, pl.ds(col, 256)], Hs.at[me, :, pl.ds(gi * 256, 256)], 5,
                dev(xs, z, zh, cs))

    wait_for(Wg.at[pl.ds(0, 3)], rsem.at[17])
    wait_for(Hf.at[0], lsem.at[0])
    wait_for(Hf.at[0], rsem.at[21])
    w_all = Wg[...].reshape(2048, HD)
    Vp[...] = jnp.dot(Hf[1 - c], w_all, preferred_element_type=F32)
    put(Vp, Vs, 8, sib)
    own_part = jnp.dot(Hf[c], w_all, preferred_element_type=F32)
    wait_for(Vs, rsem.at[8])
    val = (own_part + Vs[...]).astype(BF)

    @pl.when(main)
    def _():
        rows = pl.ds(pl.multiple_of(z * TOK, TOK), TOK)
        Vb[rows, :] = val
        for zz in line:
            put(Vb.at[rows, :], Vb.at[rows, :], 11, dev(x, zz, zh, 0))

    @pl.when(trace)
    def _():
        @pl.when(c == 0)
        def _():
            wait_for(Cb.at[0], lsem.at[3])

        wait_for(Cb.at[pl.ds(0, 3)], rsem.at[6])
        wait_for(ML.at[pl.ds(0, 3)], rsem.at[7])

        def scale_block(xq, carry):
            parts = [ML[s, xq] for s in range(NX)]
            high = functools.reduce(jnp.maximum, [p[0:2] for p in parts])
            total = functools.reduce(
                jnp.add, [p[2:4] * jnp.exp2(p[0:2] - high) for p in parts])
            w = jnp.exp2(ML[x, xq][0:2] - high) / total
            Wr[xq] = jnp.concatenate([w, jnp.zeros((6, 256), F32)], axis=0)
            for pair in range(2):
                cp = stack_pair(Cb[xq, :, pl.ds(pair * 256, 256)]).astype(F32)
                rows = pl.ds(pl.multiple_of(xq * 512 + pair * 256, 256), 256)
                Cs[rows, :] = (cp * flip(w[pair:pair + 1], TOK)).astype(BF)
            return carry

        lax.fori_loop(0, NX, scale_block, 0)
        theirs = pl.ds(pl.multiple_of((1 - c) * 512, 512), 512)
        ours = pl.ds(half, 512)
        Tsend[...] = jnp.dot(Pm[theirs, :], Cs[...], preferred_element_type=F32).astype(BF)
        put(Tsend, Tsib, 9, sib)
        mine = jnp.dot(Pm[ours, :], Cs[...], preferred_element_type=F32)
        wait_for(Tsib, rsem.at[9])
        Tz[...] = (mine + Tsib[...].astype(F32)).astype(BF).reshape(4, TOK, HD)
        for k in range(4):
            zt = 4 * c + k

            @pl.when(zt != z)
            def _():
                put(Tz.at[k], Tr.at[z], 10, dev(x, zt, zh, c))

            @pl.when(zt == z)
            def _():
                Tr[z] = Tz[k]

    @pl.when(local)
    def _():
        wait_for(Qf, lsem.at[4])
        wait_for(Cf, lsem.at[5])
        val_t = jnp.transpose(val)
        d_row = docv[...].astype(F32)
        seen = jnp.logical_and(flip(p_row, TOK) <= p_row, flip(d_row, TOK) == d_row)
        terms = jnp.zeros((TOK, HD), F32)
        for pair in range(4):
            qp = stack_pair(Qf[:, pl.ds(pair * 256, 256)])
            s = lax.dot_general(Kv[pl.ds(0, TOK), :], qp, NT, preferred_element_type=F32)
            s = jnp.concatenate(
                [jnp.where(seen, s[:, :HD], HIDDEN), jnp.where(seen, s[:, HD:], HIDDEN)], axis=1)
            s = s * SCALE
            p = jnp.exp2(s - jnp.max(s, axis=0, keepdims=True))
            w = 1.0 / jnp.sum(p, axis=0, keepdims=True)
            pb = (p * w).astype(BF)
            o = jnp.dot(val_t, pb, preferred_element_type=F32)
            att[:, pl.ds(pair * 256, HD)] = jnp.transpose(o[:, :HD]).astype(BF)
            att[:, pl.ds(pair * 256 + HD, HD)] = jnp.transpose(o[:, HD:]).astype(BF)
            cp = stack_pair(Cf[:, pl.ds(pair * 256, 256)])
            terms = terms + jnp.dot(pb, cp, preferred_element_type=F32)
        Vg[me] = terms.astype(BF)
        for phase, core in ((12, 0), (13, 1)):
            @pl.when(c == core)
            def _():
                for xs, cs in near:
                    put(Vg.at[me], Vg.at[me], phase, dev(xs, z, zh, cs))

    @pl.when(main)
    def _():
        wait_for(Vb.at[pl.ds(0, 7 * TOK), :], rsem.at[11])
        put(Vb, Vb, 18, sib)

    wait_for(Hs.at[pl.ds(0, 7)], rsem.at[5])
    wait_for(Hs.at[0], lsem.at[1])
    for s in range(8):
        HsT[:, pl.ds(s * TOK, TOK)] = jnp.transpose(Hs[s])

    @pl.when(trace_owner)
    def _():
        wait_for(Tr.at[pl.ds(0, 7)], rsem.at[10])
        Vg[2 * x] = functools.reduce(
            jnp.add, [Tr[s].astype(F32) for s in range(NZ)]).astype(BF)
        for xs, cs in near:
            put(Vg.at[2 * x], Vg.at[2 * x], 12, dev(xs, z, zh, cs))

    @pl.when(trace)
    def _():
        @pl.when(c == 1)
        def _():
            wait_for(Vb, rsem.at[18])

        VT[...] = jnp.transpose(Vb[...])

        def out_block(xq, carry):
            w = Wr[xq]
            for pair in range(2):
                at = pl.ds(pl.multiple_of(xq * 512 + pair * 256, 256), 256)
                o = jnp.dot(VT[...], Pm[:, at], preferred_element_type=F32) * w[pair:pair + 1]
                Ost[xq, pl.ds(pair * 256, 256), :] = jnp.transpose(o).astype(BF)
            return carry

        lax.fori_loop(0, NX, out_block, 0)
        for xt in ring:
            put(Ost.at[xt], Or.at[x], 15, dev(xt, z, zh, c))
        Or[x] = Ost[x]

    for phase, sender in ((12, owner), (13, c == 1)):
        @pl.when(sender)
        def _():
            wait_for(Vg.at[pl.ds(0, 3)], rsem.at[phase])

        @pl.when(jnp.logical_not(sender))
        def _():
            wait_for(Vg.at[pl.ds(0, 4)], rsem.at[phase])

    vg_all = Vg[...].reshape(8 * TOK, HD)
    Gst[...] = jnp.dot(HsT[...], vg_all, preferred_element_type=F32).astype(BF).reshape(16, 32, HD)

    @pl.when(trace)
    def _():
        pl.semaphore_wait(far_in, NZ)

    for k in (8, 7, 9, 6, 10, 5, 11, 4, 12, 3, 13, 2, 14, 1, 15):
        zz = (z16 + k) % 16
        put(Gst.at[zz], Gr.at[z16], 14, dev(x, zz % NZ, zz // NZ, c))
    Gr[z16] = Gst[z16]

    @pl.when(trace)
    def _():
        wait_for(Or.at[pl.ds(0, 3)], rsem.at[15])
        for h in range(4):
            o = functools.reduce(
                jnp.add, [Or[s, pl.ds(h * TOK, TOK), :].astype(F32) for s in range(NX)])
            Ah[:, pl.ds(h * HD, HD)] = o.astype(BF)

        @pl.when(c == 1)
        def _():
            put(Ah, att.at[:, pl.ds(512, 512)], 22, sib)

        @pl.when(c == 0)
        def _():
            att[:, pl.ds(0, 512)] = Ah[...]
            wait_for(Ah, rsem.at[22])

    wait_for(Gr.at[pl.ds(0, 15)], rsem.at[14])
    grad[...] = functools.reduce(jnp.add, [Gr[s].astype(F32) for s in range(16)])

    @pl.when(main)
    def _():
        wait_for(Kx.at[pl.ds(0, 7)], ssem.at[0])
        wait_for(Kx, ssem.at[16])
        wait_for(Qpos, ssem.at[3])
        wait_for(Qb.at[0], ssem.at[19])
        wait_for(Cb.at[0], ssem.at[20])
        wait_for(Vb.at[pl.ds(0, 7 * TOK), :], ssem.at[11])
        wait_for(Vb, ssem.at[18])

    @pl.when(side)
    def _():
        wait_for(Ah, ssem.at[22])

    @pl.when(half_owner)
    def _():
        wait_for(Vg.at[pl.ds(0, 7)], ssem.at[4])

    wait_for(Wg.at[pl.ds(0, 3)], ssem.at[17])
    wait_for(Hf.at[0], ssem.at[21])
    wait_for(Hs.at[pl.ds(0, 7)], ssem.at[5])
    wait_for(Vp, ssem.at[8])

    @pl.when(trace)
    def _():
        wait_for(Qb.at[pl.ds(0, 3)], ssem.at[2])
        wait_for(Cb.at[pl.ds(0, 3)], ssem.at[6])
        wait_for(ML.at[pl.ds(0, 3)], ssem.at[7])
        wait_for(Tsend, ssem.at[9])
        wait_for(Or.at[pl.ds(0, 3)], ssem.at[15])

    @pl.when(trace_owner)
    def _():
        wait_for(Tz.at[pl.ds(0, 3)], ssem.at[10])

    @pl.when(jnp.logical_and(trace, jnp.logical_not(trace_owner)))
    def _():
        wait_for(Tz, ssem.at[10])

    @pl.when(owner)
    def _():
        wait_for(Vg.at[pl.ds(0, 7)], ssem.at[12])

    @pl.when(c == 1)
    def _():
        wait_for(Vg.at[pl.ds(0, 7)], ssem.at[13])

    wait_for(Gr.at[pl.ds(0, 15)], ssem.at[14])


def per_device(hidden_in, value_weight, queries, key_vectors, cotangent, doc_ids, positions):
    vmem = pl.BlockSpec(memory_space=pltpu.VMEM)
    hbm = pl.BlockSpec(memory_space=pltpu.HBM)
    scratch = [
        pltpu.VMEM((1, TOK), jnp.int32),
        pltpu.VMEM((1, TOK), jnp.int32),
        pltpu.VMEM((8, TOK), jnp.int32),
        pltpu.VMEM((TOK + 16, HD), BF),
        pltpu.VMEM((NX, 512, HD), BF),
        pltpu.VMEM((2, TOK, 2048), BF),
        pltpu.VMEM((8, TOK, 512), BF),
        pltpu.VMEM((512, 1024), BF),
        pltpu.VMEM((NZ, TOK + 16, HD), BF),
        pltpu.VMEM((1024, TOK), F32),
        pltpu.VMEM((NX, TOK, 512), BF),
        pltpu.VMEM((7, 8, TOK), jnp.int32),
        pltpu.VMEM((NX, TOK, 512), BF),
        pltpu.VMEM((TOK, 1024), BF),
        pltpu.VMEM((TOK, 1024), BF),
        pltpu.VMEM((1024, 256), F32),
        pltpu.VMEM((1024, 2048), BF),
        pltpu.VMEM((NX, NX, 8, 256), F32),
        pltpu.VMEM((NX, 8, 256), F32),
        pltpu.VMEM((2048, HD), BF),
        pltpu.VMEM((TOK, HD), F32),
        pltpu.VMEM((TOK, HD), F32),
        pltpu.VMEM((1024, HD), BF),
        pltpu.VMEM((HD, 1024), BF),
        pltpu.VMEM((512, HD), BF),
        pltpu.VMEM((512, HD), BF),
        pltpu.VMEM((4, TOK, HD), BF),
        pltpu.VMEM((8, TOK, HD), BF),
        pltpu.VMEM((8, TOK, HD), BF),
        pltpu.VMEM((NX, 512, HD), BF),
        pltpu.VMEM((NX, 512, HD), BF),
        pltpu.VMEM((TOK, 512), BF),
        pltpu.VMEM((16, 32, HD), BF),
        pltpu.VMEM((16, 32, HD), BF),
        pltpu.SemaphoreType.DMA((23,)),
        pltpu.SemaphoreType.DMA((23,)),
        pltpu.SemaphoreType.DMA((9,)),
        pltpu.SemaphoreType.REGULAR,
    ]
    return pl.pallas_call(
        kernel,
        name="trace_attention",
        out_shape=(
            jax.ShapeDtypeStruct((TOK, 1024), BF),
            jax.ShapeDtypeStruct((32, HD), F32),
        ),
        in_specs=[hbm] * 7,
        out_specs=(vmem, vmem),
        scratch_shapes=scratch,
        compiler_params=pltpu.CompilerParams(
            collective_id=0, has_side_effects=True, vmem_limit_bytes=56 << 20
        ),
    )(
        hidden_in, value_weight, queries, key_vectors, cotangent,
        doc_ids.reshape(1, TOK), positions.reshape(1, TOK),
    )


def solution(mesh):
    in_specs = (
        P(("grp", "blk"), None),
        P("blk", "tp"),
        P(("grp", "blk"), "tp"),
        P(("grp", "blk"), "tp"),
        P(("grp", "blk"), "tp"),
        P(("grp", "blk")),
        P(("grp", "blk")),
    )
    out_specs = (P(("grp", "blk"), "tp"), P(("grp", "blk"), "tp"))
    return jax.shard_map(
        per_device, mesh=mesh, in_specs=in_specs, out_specs=out_specs, check_vma=False
    )
```
